128 devices in a mesh: grp: 4 (over z), row: 32 (over y, x, core).
Axes of the slice: x: 4, y: 4, z: 4, core: 2. Of those that a mesh axis runs over, the one named last changes fastest.
Arguments:
- momentum: bfloat16 [8, 7168, 2048], P('grp', 'row')
- gradient: bfloat16 [8, 7168, 2048], P('grp', 'row'), may hold values from -4 to 4
- qfactor: bfloat16 [16, 2048, 512], P('grp'), may hold values from -6 to 6
- owner_of: int32 [8], replicated, may hold values from 0 to 3, as said below
Outputs:
- new_momentum: bfloat16 [8, 7168, 2048], P('grp', 'row')
- update: bfloat16 [8, 7168, 2048], P('grp', 'row')
- new_qfactor: bfloat16 [16, 2048, 512], P('grp')
The draws below stay inside these ranges and needn't reach their ends.
Inputs may be any that keep to these rules, and one draw needn't show every extreme that they name: `owner_of`: matrix e is homed on group e // 2. Of the 2 matrices homed on one group at most 1 have the same owner, and in every draw one group owns exactly 4 matrices, 1 from each home group. Slots of qfactor beyond a group's count are not read.
All inputs are finite; a program needn't handle non-finite values.
Results may differ from the reference program's by a relative error of at most 0.019.
Values may be sent and summed in bfloat16 or wider, within the bound.
No kernel may reach another device: no remote copies, remote signals or barrier semaphores. Data moves between devices by JAX's collectives and lax.ppermute only.
A program may use at most 192 MiB of HBM per device.

```python
import math
import jax
import jax.numpy as jnp
from jax import lax

MODEL_DIM = 7168
EXPERT_DIM = 2048
RANK = 512
HOMED = 2
PAIR_MOST = 1
OWNED_MOST = 4
EXPERTS = 8
SLOTS = 16
N_GRP = 4


def draw_momentum(key, part):
    key = jax.random.fold_in(key, 11)
    first, second, third = jax.random.split(key, 3)
    column = jnp.arange(EXPERT_DIM, dtype=jnp.float32) / EXPERT_DIM
    base = jax.random.normal(first, (EXPERTS, MODEL_DIM, EXPERT_DIM), jnp.float32)
    rising = jnp.exp(jnp.log(10.0) * column)
    jitter = jnp.exp(0.5 * jax.random.uniform(second, (EXPERTS, 1, EXPERT_DIM), jnp.float32, -1.0, 1.0))
    rowwise = jnp.exp(0.3 * jax.random.uniform(third, (EXPERTS, MODEL_DIM, 1), jnp.float32, -1.0, 1.0))
    return (base * rising[None, None, :] * jitter * rowwise).astype(jnp.bfloat16)


def draw_owner_of(key, part):
    key = jax.random.fold_in(key, 7)
    first, second, third = jax.random.split(key, 3)
    busiest = jax.random.randint(first, (), 0, N_GRP)
    keys = jax.random.split(second, N_GRP)
    orders = jax.vmap(lambda k: jax.random.permutation(k, HOMED))(keys)
    places = jnp.argsort(orders, axis=1)
    others = (busiest + 1 + jax.random.randint(third, (N_GRP, HOMED), 0, N_GRP - 1)) % N_GRP
    owners = jnp.where(places < PAIR_MOST, busiest, others)
    return owners.reshape(-1).astype(jnp.int32)


def steps_of(rng, extent, pieces, low, high):
    factor_of = 1.0
    for dim, blocks in pieces:
        steps = jax.random.uniform(jax.random.fold_in(jax.random.fold_in(rng, 6), dim), (blocks,), jnp.float32, low / len(pieces), high / len(pieces))
        factor_of = factor_of * jnp.repeat(jnp.exp(steps), extent[dim] // blocks).reshape((-1,) + (1,) * (len(extent) - 1 - dim))
    return factor_of


def scatter_about(rng, dims, width, bound, cuts=(), kind=jnp.bfloat16):
    entries = jax.random.normal(rng, dims, jnp.float32) * width
    if len(cuts) > 0:
        entries = steps_of(rng, dims, cuts, -0.22, 0.18) * entries
    return jnp.clip(entries, min=-bound, max=bound).astype(kind)


def setup_inputs(seed: int = 0) -> dict:
    arg_keys = jax.random.split(jax.random.key(seed), 5)
    return {
        "momentum": draw_momentum(jax.random.fold_in(arg_keys[4], 71), 0),
        "gradient": scatter_about(arg_keys[1], (EXPERTS, MODEL_DIM, EXPERT_DIM), 0.3, 4.0, ((0, 4), (1, 32))),
        "qfactor": scatter_about(arg_keys[2], (SLOTS, EXPERT_DIM, RANK), 1.0, 6.0, ((0, 4),)),
        "owner_of": draw_owner_of(jax.random.fold_in(arg_keys[4], 71), 0),
    }


momentum_decay = 0.95
root_eps = 1e-06

def reference(momentum, gradient, qfactor, owner_of):
    index = jnp.arange(EXPERTS, dtype=jnp.int32)
    same = owner_of[:, None] == owner_of[None, :]
    earlier = index[None, :] < index[:, None]
    slot = lax.optimization_barrier(jnp.sum((same & earlier).astype(jnp.int32), axis=1))
    target = (owner_of * OWNED_MOST + slot).astype(jnp.int32)

    def single(expert):
        blended = (momentum_decay * momentum[expert].astype(jnp.float32) + gradient[expert].astype(jnp.float32)).astype(jnp.bfloat16)
        right = qfactor[target[expert]]
        proj = jnp.dot(blended.astype(jnp.float32), right.astype(jnp.float32), preferred_element_type=jnp.float32)
        gram = jnp.dot(proj.T, proj, precision=lax.Precision.HIGHEST)
        lower = jnp.linalg.cholesky(gram)
        basis = jax.scipy.linalg.solve_triangular(lower, proj.T, lower=True).T.astype(jnp.bfloat16)
        summed = jnp.dot(blended.T.astype(jnp.float32), basis.astype(jnp.float32), preferred_element_type=jnp.float32)
        scaling = lax.rsqrt(lax.optimization_barrier(jnp.mean(summed * summed, axis=0)) + root_eps)
        rounded = summed.astype(jnp.bfloat16)
        fresh = (rounded.astype(jnp.float32) * scaling[None, :]).astype(jnp.bfloat16)
        kept = (blended.astype(jnp.float32) - (1.0 - momentum_decay) * jnp.dot(basis.astype(jnp.float32), rounded.T.astype(jnp.float32), preferred_element_type=jnp.float32)).astype(jnp.bfloat16)
        factor = math.sqrt(MODEL_DIM * EXPERT_DIM / RANK)
        update = (factor * jnp.dot(basis.astype(jnp.float32), fresh.T.astype(jnp.float32), preferred_element_type=jnp.float32)).astype(jnp.bfloat16)
        return (kept, update, fresh)
    kept_all, update_all, fresh_all = lax.map(single, index)
    new_qfactor = jnp.zeros((SLOTS, EXPERT_DIM, RANK), jnp.bfloat16).at[target].set(fresh_all)
    return (kept_all, update_all, new_qfactor)
```

```python
import math

import jax
import jax.numpy as jnp
from jax import lax
from jax.experimental import pallas as pl
from jax.experimental.pallas import tpu as pltpu
from jax.sharding import Mesh
from jax.sharding import PartitionSpec as P

momentum_decay = 0.95
root_eps = 1e-06
HIGHEST = lax.Precision.HIGHEST
F32 = jnp.float32
BF16 = jnp.bfloat16
PLANE = ("y", "x")
ROWS = ("y", "x", "core")
BLOCK = 128


def eliminate(block):
    size = block.shape[0]
    lane = lax.broadcasted_iota(jnp.int32, (8, size), 1)
    sub = lax.broadcasted_iota(jnp.int32, (8, size), 0)
    tiles = [block[8 * t : 8 * t + 8, :] for t in range(size // 8)]
    for k in range(size):
        first, at = k // 8, k % 8
        columns = [jnp.broadcast_to(tile[:, k : k + 1], (8, size)) for tile in tiles[first:]]
        inverse = 1.0 / columns[0][at : at + 1, :]
        row = tiles[first][at : at + 1, :]
        scaled = jnp.where(lane[0:1] == k, inverse, row * inverse)
        scaled = jnp.broadcast_to(scaled, (8, size))
        for t in range(first, size // 8):
            new = jnp.where(lane == k, 0.0, tiles[t]) - columns[t - first] * scaled
            if t == first:
                new = jnp.where(sub > at, new, tiles[t])
            tiles[t] = new
    full = jnp.concatenate(tiles, axis=0)
    r = lax.broadcasted_iota(jnp.int32, (size, size), 0)
    c = lax.broadcasted_iota(jnp.int32, (size, size), 1)
    pivots = jnp.sum(jnp.where(r == c, full, 0.0), axis=1, keepdims=True)
    return jnp.where(r > c, full, jnp.where(r == c, 1.0, 0.0)) * lax.rsqrt(pivots)


def dot(a, b, turned=False):
    return lax.dot_general(
        a,
        b,
        (((1,), (1 if turned else 0,)), ((), ())),
        precision=HIGHEST,
        preferred_element_type=F32,
    )


def factor_kernel(gram_ref, out_ref, work_ref):
    size = work_ref.shape[0]
    steps = size // BLOCK
    place = 0
    for i in range(steps):
        for j in range(i + 1):
            piece = gram_ref[place]
            work_ref[i * BLOCK : (i + 1) * BLOCK, j * BLOCK : (j + 1) * BLOCK] = piece
            place += 1
    for j in range(steps):
        lo, hi = j * BLOCK, (j + 1) * BLOCK
        inverse = eliminate(work_ref[lo:hi, lo:hi])
        out_ref[lo:hi, lo:hi] = inverse
        if j > 0:
            out_ref[lo:hi, :lo] = dot(inverse, work_ref[lo:hi, :lo])
        if j < steps - 1:
            out_ref[lo:hi, hi:] = jnp.zeros((BLOCK, size - hi), F32)
            low = dot(work_ref[hi:, lo:hi], inverse, turned=True)
            if j > 0:
                work_ref[hi:, :lo] -= dot(low, out_ref[lo:hi, :lo])
            work_ref[hi:, lo:hi] = -dot(low, inverse)
            work_ref[hi:, hi:] -= dot(low, low, turned=True)


def inverse_factor(packed, rank):
    return pl.pallas_call(
        factor_kernel,
        out_shape=jax.ShapeDtypeStruct((rank, rank), F32),
        scratch_shapes=[pltpu.VMEM((rank, rank), F32)],
        compiler_params=pltpu.CompilerParams(vmem_limit_bytes=32 * 1024 * 1024),
        cost_estimate=pl.CostEstimate(
            flops=40_000_000_000, bytes_accessed=2 * 1024 * 1024, transcendentals=0
        ),
        name="inverse_factor",
    )(packed)


def swap_core(x):
    return lax.ppermute(x, "core", [(0, 1), (1, 0)])


def shift_group(x, k):
    n = lax.axis_size("grp")
    return lax.ppermute(x, "grp", [(i, (i + k) % n) for i in range(n)])


def gather_plane(x):
    chips = lax.axis_size(PLANE)
    many = jnp.broadcast_to(x[None], (chips,) + x.shape)
    return lax.all_to_all(many, PLANE, 0, 0, tiled=True)


def scatter_plane(x):
    chips = lax.axis_size(PLANE)
    parts = x.reshape((chips, x.shape[0] // chips) + x.shape[1:])
    return jnp.sum(lax.all_to_all(parts, PLANE, 0, 0, tiled=True), axis=0)


def local(momentum, gradient, qfactor, owner_of):
    groups = lax.axis_size("grp")
    chips = lax.axis_size(PLANE)
    homed, rows_local, width = momentum.shape
    owned, unused, rank = qfactor.shape
    total = owner_of.shape[0]
    group = lax.axis_index("grp")
    core = lax.axis_index("core")
    chip = lax.axis_index(PLANE)

    index = jnp.arange(total, dtype=jnp.int32)
    same = owner_of[:, None] == owner_of[None, :]
    earlier = index[None, :] < index[:, None]
    slot = jnp.sum((same & earlier).astype(jnp.int32), axis=1)

    share = width // chips
    right = jnp.zeros((share, rank), BF16)
    mine = group * homed + core
    for k in range(groups):
        target = lax.rem(group + k, groups) * homed + core
        piece = lax.dynamic_slice(
            qfactor, (slot[target], chip * share, 0), (1, share, rank)
        )[0]
        if k > 0:
            piece = shift_group(piece, k)
        source = lax.rem(group - k + groups, groups)
        right = jnp.where(owner_of[mine] == source, piece, right)
    right = gather_plane(right).reshape(width, rank)

    blended = (momentum_decay * momentum.astype(F32) + gradient.astype(F32)).astype(BF16)
    keep = jnp.where(core == 0, blended[0], blended[1])
    give = jnp.where(core == 0, blended[1], blended[0])
    block = jnp.concatenate([keep, swap_core(give)], axis=0)

    proj = jnp.dot(block, right, preferred_element_type=F32)
    gram = lax.dot_general(proj, proj, (((0,), (0,)), ((), ())), precision=HIGHEST)
    steps = rank // BLOCK
    packed = jnp.concatenate(
        [
            gram[i * BLOCK : (i + 1) * BLOCK, j * BLOCK : (j + 1) * BLOCK]
            for i in range(steps)
            for j in range(i + 1)
        ],
        axis=0,
    )
    packed = gather_plane(scatter_plane(packed)).reshape(-1, BLOCK, BLOCK)
    inverse = inverse_factor(packed, rank)

    high = proj.astype(BF16)
    rest = proj - high.astype(F32)
    mid = rest.astype(BF16)
    low = (rest - mid.astype(F32)).astype(BF16)
    cross = sum(
        lax.dot_general(block, part, (((0,), (0,)), ((), ())), preferred_element_type=F32)
        for part in (low, mid, high)
    )
    cross = scatter_plane(cross)

    summed = dot(cross, inverse, turned=True)
    rounded = summed.astype(BF16)
    basis = dot(proj, inverse, turned=True).astype(BF16)

    half = share // 2
    lower, upper = rounded[:half], rounded[half:]
    stay = jnp.where(core == 0, lower, upper)
    other = swap_core(jnp.where(core == 0, upper, lower))
    first = jnp.where(core == 0, stay, other)
    second = jnp.where(core == 0, other, stay)
    arrived = []
    for k in range(groups):
        target = lax.rem(group + k, groups)
        piece = jnp.where(owner_of[group * homed] == target, first, second)
        arrived.append(shift_group(piece, k) if k > 0 else piece)
    slots = []
    for s in range(owned):
        value = jnp.zeros((half, rank), BF16)
        for k in range(groups):
            source = lax.rem(group - k + groups, groups)
            for h in range(homed):
                e = source * homed + h
                hit = (owner_of[e] == group) & (slot[e] == s)
                value = jnp.where(hit, arrived[k], value)
        slots.append(value)
    slots = jnp.stack(slots)
    owners = lax.all_gather(slots, ROWS, axis=1, tiled=True)
    squares = jnp.mean(jnp.square(owners.astype(F32)), axis=1, keepdims=True)
    new_qfactor = (owners.astype(F32) * lax.rsqrt(squares + root_eps)).astype(BF16)

    full = gather_plane(rounded).reshape(width, rank)
    scaling = lax.rsqrt(jnp.mean(jnp.square(full.astype(F32)), axis=0) + root_eps)
    fresh = (full.astype(F32) * scaling[None, :]).astype(BF16)
    along = (((1,), (1,)), ((), ()))
    kept = (
        block.astype(F32)
        - (1.0 - momentum_decay)
        * lax.dot_general(basis, full, along, preferred_element_type=F32)
    ).astype(BF16)
    factor = math.sqrt(2 * rows_local * chips * width / rank)
    moved = (
        factor * lax.dot_general(basis, fresh, along, preferred_element_type=F32)
    ).astype(BF16)

    def home(x):
        stay, back = x[:rows_local], swap_core(x[rows_local:])
        return jnp.where(core == 0, jnp.stack([stay, back]), jnp.stack([back, stay]))

    return (home(kept), home(moved), new_qfactor)


def solution(mesh):
    fine = Mesh(mesh.devices.reshape(4, 4, 4, 2), ("grp", "y", "x", "core"))
    rows = P("grp", ROWS, None)
    return jax.shard_map(
        local,
        mesh=fine,
        in_specs=(rows, rows, P("grp", None, None), P()),
        out_specs=(rows, rows, P("grp", None, None)),
        check_vma=False,
    )
```

```python
import math

import jax
import jax.numpy as jnp
from jax import lax
from jax.experimental import pallas as pl
from jax.experimental.pallas import tpu as pltpu
from jax.sharding import Mesh
from jax.sharding import PartitionSpec as P

momentum_decay = 0.95
root_eps = 1e-06
HIGHEST = lax.Precision.HIGHEST
F32 = jnp.float32
BF16 = jnp.bfloat16
PLANE = ("y", "x")
ROWS = ("y", "x", "core")
BLOCK = 128


def eliminate(block):
    size = block.shape[0]
    lane = lax.broadcasted_iota(jnp.int32, (8, size), 1)
    sub = lax.broadcasted_iota(jnp.int32, (8, size), 0)
    tiles = [block[8 * t : 8 * t + 8, :] for t in range(size // 8)]
    for k in range(size):
        first, at = k // 8, k % 8
        columns = [jnp.broadcast_to(tile[:, k : k + 1], (8, size)) for tile in tiles[first:]]
        inverse = 1.0 / columns[0][at : at + 1, :]
        row = tiles[first][at : at + 1, :]
        scaled = jnp.where(lane[0:1] == k, inverse, row * inverse)
        scaled = jnp.broadcast_to(scaled, (8, size))
        for t in range(first, size // 8):
            new = jnp.where(lane == k, 0.0, tiles[t]) - columns[t - first] * scaled
            if t == first:
                new = jnp.where(sub > at, new, tiles[t])
            tiles[t] = new
    full = jnp.concatenate(tiles, axis=0)
    r = lax.broadcasted_iota(jnp.int32, (size, size), 0)
    c = lax.broadcasted_iota(jnp.int32, (size, size), 1)
    pivots = jnp.sum(jnp.where(r == c, full, 0.0), axis=1, keepdims=True)
    return jnp.where(r > c, full, jnp.where(r == c, 1.0, 0.0)) * lax.rsqrt(pivots)


def dot(a, b, turned=False):
    return lax.dot_general(
        a,
        b,
        (((1,), (1 if turned else 0,)), ((), ())),
        precision=HIGHEST,
        preferred_element_type=F32,
    )


def factor_kernel(gram_ref, out_ref, work_ref):
    size = work_ref.shape[0]
    steps = size // BLOCK
    place = 0
    for i in range(steps):
        for j in range(i + 1):
            piece = gram_ref[place]
            work_ref[i * BLOCK : (i + 1) * BLOCK, j * BLOCK : (j + 1) * BLOCK] = piece
            place += 1
    for j in range(steps):
        lo, hi = j * BLOCK, (j + 1) * BLOCK
        inverse = eliminate(work_ref[lo:hi, lo:hi])
        out_ref[lo:hi, lo:hi] = inverse
        if j > 0:
            out_ref[lo:hi, :lo] = dot(inverse, work_ref[lo:hi, :lo])
        if j < steps - 1:
            out_ref[lo:hi, hi:] = jnp.zeros((BLOCK, size - hi), F32)
            low = dot(work_ref[hi:, lo:hi], inverse, turned=True)
            if j > 0:
                work_ref[hi:, :lo] -= dot(low, out_ref[lo:hi, :lo])
            work_ref[hi:, lo:hi] = -dot(low, inverse)
            work_ref[hi:, hi:] -= dot(low, low, turned=True)


def inverse_factor(packed, rank):
    return pl.pallas_call(
        factor_kernel,
        out_shape=jax.ShapeDtypeStruct((rank, rank), F32),
        scratch_shapes=[pltpu.VMEM((rank, rank), F32)],
        compiler_params=pltpu.CompilerParams(vmem_limit_bytes=32 * 1024 * 1024),
        cost_estimate=pl.CostEstimate(
            flops=40_000_000_000, bytes_accessed=2 * 1024 * 1024, transcendentals=0
        ),
        name="inverse_factor",
    )(packed)


def project_kernel(block_ref, right_ref, proj_ref, packed_ref):
    chips, share, rank = right_ref.shape
    rows, width = block_ref.shape
    right = right_ref[...].reshape(width, rank)
    proj = jnp.dot(block_ref[...], right, preferred_element_type=F32)
    proj_ref[...] = proj
    place = 0
    for i in range(rank // BLOCK):
        wide = lax.dot_general(
            proj[:, i * BLOCK : (i + 1) * BLOCK],
            proj[:, : (i + 1) * BLOCK],
            (((0,), (0,)), ((), ())),
            precision=HIGHEST,
            preferred_element_type=F32,
        )
        for j in range(i + 1):
            packed_ref[place] = wide[:, j * BLOCK : (j + 1) * BLOCK]
            place += 1


def project(block, right):
    rows, rank = block.shape[0], right.shape[2]
    steps = rank // BLOCK
    pieces = steps * (steps + 1) // 2
    return pl.pallas_call(
        project_kernel,
        out_shape=(
            jax.ShapeDtypeStruct((rows, rank), F32),
            jax.ShapeDtypeStruct((pieces, BLOCK, BLOCK), F32),
        ),
        compiler_params=pltpu.CompilerParams(vmem_limit_bytes=32 * 1024 * 1024),
        cost_estimate=pl.CostEstimate(
            flops=4_000_000_000, bytes_accessed=5 * 1024 * 1024, transcendentals=0
        ),
        name="project",
    )(block, right)


def normalise_kernel(in_ref, out_ref):
    width = in_ref.shape[1]
    piece = 256

    def add(i, total):
        value = in_ref[0, pl.ds(i * piece, piece), :].astype(F32)
        return total + jnp.sum(value * value, axis=0, keepdims=True)

    total = lax.fori_loop(
        0, width // piece, add, jnp.zeros((1, in_ref.shape[2]), F32), unroll=True
    )
    scaling = lax.rsqrt(total / width + root_eps)

    def write(i, carry):
        at = pl.ds(i * piece, piece)
        out_ref[0, at, :] = (in_ref[0, at, :].astype(F32) * scaling).astype(BF16)
        return carry

    lax.fori_loop(0, width // piece, write, 0, unroll=True)


def normalise(x):
    spec = pl.BlockSpec((1,) + x.shape[1:], lambda s: (s, 0, 0))
    return pl.pallas_call(
        normalise_kernel,
        grid=(x.shape[0],),
        in_specs=[spec],
        out_specs=spec,
        out_shape=jax.ShapeDtypeStruct(x.shape, x.dtype),
        compiler_params=pltpu.CompilerParams(vmem_limit_bytes=32 * 1024 * 1024),
        cost_estimate=pl.CostEstimate(
            flops=20_000_000, bytes_accessed=2 * x.size * 2, transcendentals=0
        ),
        name="normalise",
    )(x)


def swap_core(x):
    return lax.ppermute(x, "core", [(0, 1), (1, 0)])


def shift_group(x, k):
    n = lax.axis_size("grp")
    return lax.ppermute(x, "grp", [(i, (i + k) % n) for i in range(n)])


def gather_plane(x):
    chips = lax.axis_size(PLANE)
    many = jnp.broadcast_to(x[None], (chips,) + x.shape)
    return lax.all_to_all(many, PLANE, 0, 0, tiled=True)


def scatter_plane(x):
    chips = lax.axis_size(PLANE)
    parts = x.reshape((chips, x.shape[0] // chips) + x.shape[1:])
    return jnp.sum(lax.all_to_all(parts, PLANE, 0, 0, tiled=True), axis=0)


def local(momentum, gradient, qfactor, owner_of):
    groups = lax.axis_size("grp")
    chips = lax.axis_size(PLANE)
    homed, rows_local, width = momentum.shape
    owned, unused, rank = qfactor.shape
    total = owner_of.shape[0]
    group = lax.axis_index("grp")
    core = lax.axis_index("core")
    chip = lax.axis_index(PLANE)

    index = jnp.arange(total, dtype=jnp.int32)
    same = owner_of[:, None] == owner_of[None, :]
    earlier = index[None, :] < index[:, None]
    slot = jnp.sum((same & earlier).astype(jnp.int32), axis=1)
    hops = jnp.arange(groups, dtype=jnp.int32)
    after = (group + hops) % groups
    before = (group - hops + groups) % groups
    slots = jnp.arange(owned, dtype=jnp.int32)
    house = index // homed
    in_slot = (slot[:, None] == slots[None, :]) & (owner_of == group)[:, None]
    this_core = index % homed == core

    share = width // chips
    held = lax.dynamic_slice(qfactor, (0, chip * share, 0), (owned, share, rank))
    goes = (house[None, :] == after[:, None]) & this_core[None, :]
    goes = jnp.any(goes[:, :, None] & in_slot[None, :, :], axis=1)
    comes = (house == group) & this_core
    comes = jnp.any(comes[None, :] & (owner_of[None, :] == before[:, None]), axis=1)
    pieces = []
    for k in range(groups):
        piece = jnp.sum(jnp.where(goes[k][:, None, None], held, 0), axis=0, dtype=BF16)
        pieces.append(shift_group(piece, k) if k > 0 else piece)
    right = jnp.sum(
        jnp.where(comes[:, None, None], jnp.stack(pieces), 0), axis=0, dtype=BF16
    )
    right = gather_plane(right)

    blended = (momentum_decay * momentum.astype(F32) + gradient.astype(F32)).astype(BF16)
    keep = jnp.where(core == 0, blended[0], blended[1])
    give = jnp.where(core == 0, blended[1], blended[0])
    block = jnp.concatenate([keep, swap_core(give)], axis=0)

    proj, packed = project(block, right)
    packed = packed.reshape(-1, BLOCK)
    packed = gather_plane(scatter_plane(packed)).reshape(-1, BLOCK, BLOCK)
    inverse = inverse_factor(packed, rank)

    high = proj.astype(BF16)
    rest = proj - high.astype(F32)
    mid = rest.astype(BF16)
    low = (rest - mid.astype(F32)).astype(BF16)
    cross = sum(
        lax.dot_general(block, part, (((0,), (0,)), ((), ())), preferred_element_type=F32)
        for part in (low, mid, high)
    )
    cross = scatter_plane(cross)

    summed = dot(cross, inverse, turned=True)
    rounded = summed.astype(BF16)
    basis = dot(proj, inverse, turned=True).astype(BF16)

    half = share // 2
    lower, upper = rounded[:half], rounded[half:]
    stay = jnp.where(core == 0, lower, upper)
    other = swap_core(jnp.where(core == 0, upper, lower))
    first = jnp.where(core == 0, stay, other)
    second = jnp.where(core == 0, other, stay)
    theirs = (house == group)[None, :] & (owner_of[None, :] == after[:, None])
    theirs = jnp.any(theirs & (index % homed == 0)[None, :], axis=1)
    arrived = []
    for k in range(groups):
        piece = jnp.where(theirs[k : k + 1, None], first, second)
        arrived.append(shift_group(piece, k) if k > 0 else piece)
    place = jnp.any(
        in_slot[:, :, None] & (house[:, None, None] == before[None, None, :]), axis=0
    )
    stacked = jnp.stack(arrived)
    filled = jnp.stack(
        [
            jnp.sum(jnp.where(place[s][:, None, None], stacked, 0), axis=0, dtype=BF16)
            for s in range(owned)
        ]
    )
    new_qfactor = normalise(lax.all_gather(filled, ROWS, axis=1, tiled=True))

    full = gather_plane(rounded).reshape(width, rank)
    scaling = lax.rsqrt(jnp.mean(jnp.square(full.astype(F32)), axis=0) + root_eps)
    fresh = (full.astype(F32) * scaling[None, :]).astype(BF16)
    along = (((1,), (1,)), ((), ()))
    kept = (
        block.astype(F32)
        - (1.0 - momentum_decay)
        * lax.dot_general(basis, full, along, preferred_element_type=F32)
    ).astype(BF16)
    factor = math.sqrt(2 * rows_local * chips * width / rank)
    moved = (
        factor * lax.dot_general(basis, fresh, along, preferred_element_type=F32)
    ).astype(BF16)

    def home(x):
        stay, back = x[:rows_local], swap_core(x[rows_local:])
        return jnp.where(core == 0, jnp.stack([stay, back]), jnp.stack([back, stay]))

    return (home(kept), home(moved), new_qfactor)


def solution(mesh):
    fine = Mesh(mesh.devices.reshape(4, 4, 4, 2), ("grp", "y", "x", "core"))
    rows = P("grp", ROWS, None)
    return jax.shard_map(
        local,
        mesh=fine,
        in_specs=(rows, rows, P("grp", None, None), P()),
        out_specs=(rows, rows, P("grp", None, None)),
        check_vma=False,
    )
```

```python
import math

import jax
import jax.numpy as jnp
from jax import lax
from jax.experimental import pallas as pl
from jax.experimental.pallas import tpu as pltpu
from jax.sharding import Mesh
from jax.sharding import PartitionSpec as P

momentum_decay = 0.95
root_eps = 1e-06
HIGHEST = lax.Precision.HIGHEST
F32 = jnp.float32
BF16 = jnp.bfloat16
PLANE = ("y", "x")
ROWS = ("y", "x", "core")
BLOCK = 128


def eliminate(block):
    size = block.shape[0]
    lane = lax.broadcasted_iota(jnp.int32, (8, size), 1)
    sub = lax.broadcasted_iota(jnp.int32, (8, size), 0)
    count = size // 8

    def spread(tile, at):
        return jnp.broadcast_to(tile[:, at : at + 1], (8, size))

    def repeat(tile, at):
        return jnp.broadcast_to(tile[at : at + 1, :], (8, size))

    tiles = [block[8 * t : 8 * t + 8, :] for t in range(count)]
    done = []
    for t in range(count):
        base = 8 * t
        own = (lane >= base) & (lane < base + 8)
        columns = [spread(tiles[t], base + j) for j in range(8)]
        rows = jnp.where(own, jnp.where(lane == sub + base, 1.0, 0.0), tiles[t])
        result = None
        for k in range(8):
            here = sub == k
            inverse = 1.0 / repeat(columns[k], k)
            row = repeat(rows, k)
            value = row * jnp.sqrt(inverse)
            result = value if result is None else jnp.where(here, value, result)
            scaled = columns[k] * inverse
            for j in range(k + 1, 8):
                pivot = repeat(columns[j], k)
                columns[j] = jnp.where(here, pivot * inverse, columns[j] - scaled * pivot)
            rows = jnp.where(here, row * inverse, rows - scaled * row)
        done.append(jnp.where(lane <= sub + base, result, 0.0))
        solved = [repeat(rows, k) for k in range(8)]
        for u in range(t + 1, count):
            p = [spread(tiles[u], base + j) * solved[j] for j in range(8)]
            taken = ((p[0] + p[1]) + (p[2] + p[3])) + ((p[4] + p[5]) + (p[6] + p[7]))
            tiles[u] = jnp.where(own, 0.0, tiles[u]) - taken
    return jnp.concatenate(done, axis=0)


def dot(a, b, turned=False):
    return lax.dot_general(
        a,
        b,
        (((1,), (1 if turned else 0,)), ((), ())),
        precision=HIGHEST,
        preferred_element_type=F32,
    )


def product(a, b):
    return lax.dot_general(a, b, (((0,), (0,)), ((), ())), preferred_element_type=F32)


def call(kernel, name, out_shape, scratch=(), smem=0, flops=0, moved=0):
    def run(*args):
        specs = [
            pl.BlockSpec(memory_space=pltpu.SMEM if i < smem else pltpu.VMEM)
            for i in range(len(args))
        ]
        return pl.pallas_call(
            kernel,
            in_specs=specs,
            out_shape=out_shape,
            scratch_shapes=list(scratch),
            compiler_params=pltpu.CompilerParams(vmem_limit_bytes=24 * 1024 * 1024),
            cost_estimate=pl.CostEstimate(
                flops=flops, bytes_accessed=moved, transcendentals=0
            ),
            name=name,
        )(*args)

    return run


def shape(dims, dtype=F32):
    return jax.ShapeDtypeStruct(dims, dtype)


def assemble(place_ref, pieces, whole_ref):
    side = len(pieces) // 2
    share = pieces[0].shape[1]
    half = whole_ref.shape[1] // 2
    y, x = place_ref[0], place_ref[1]
    for i in range(side):
        for j in range(side):
            for part, (dy, dx) in enumerate(((i, j), (j, i))):
                chip = lax.rem(y + side - dy, side) * side + lax.rem(x + side - dx, side)
                at = pl.ds(pl.multiple_of(chip * share, share), share)
                piece = pieces[part * side + i]
                whole_ref[at, part * half : (part + 1) * half] = piece[j]


def project_kernel(place_ref, first_ref, second_ref, *refs):
    pieces, outs = refs[:8], refs[8:]
    proj_refs, part_refs, (right_ref, packed_ref) = outs[:2], outs[2:6], outs[6:]
    assemble(place_ref, pieces, right_ref)
    right = right_ref[...]
    rank = right.shape[1]
    projs = []
    for block_ref, proj_ref in zip((first_ref, second_ref), proj_refs):
        proj = jnp.dot(block_ref[...], right, preferred_element_type=F32)
        proj_ref[...] = proj
        projs.append(proj)
    place = 0
    for i in range(rank // BLOCK):
        lo, hi = i * BLOCK, (i + 1) * BLOCK
        wide = sum(
            lax.dot_general(
                proj[:, lo:hi],
                proj[:, :hi],
                (((0,), (0,)), ((), ())),
                precision=HIGHEST,
                preferred_element_type=F32,
            )
            for proj in projs
        )
        for j in range(i + 1):
            packed_ref[place * BLOCK : (place + 1) * BLOCK, :] = wide[
                :, j * BLOCK : (j + 1) * BLOCK
            ]
            place += 1
    x = place_ref[1]
    side = len(part_refs)
    rows = part_refs[0].shape[0]
    for k, part_ref in enumerate(part_refs):
        at = lax.rem(x + k, side) * rows
        part_ref[...] = packed_ref[pl.ds(pl.multiple_of(at, 8), rows), :]


def project(place, first, second, pieces):
    rows, width = first.shape
    rank = 2 * pieces[0].shape[2]
    steps = rank // BLOCK
    packed = steps * (steps + 1) // 2 * BLOCK
    out = call(
        project_kernel,
        "project",
        [shape((rows, rank))] * 2 + [shape((packed // 4, BLOCK))] * 4,
        [pltpu.VMEM((width, rank), BF16), pltpu.VMEM((packed, BLOCK), F32)],
        smem=1,
        flops=4_000_000_000,
        moved=6 * 1024 * 1024,
    )(place, first, second, *pieces)
    return out[:2], out[2:]


def add_kernel(place_ref, a_ref, b_ref, c_ref, d_ref, *refs):
    outs, total_ref = refs[:4], refs[4]
    total_ref[...] = (a_ref[...] + b_ref[...]) + (c_ref[...] + d_ref[...])
    y = place_ref[0]
    rows = outs[0].shape[0]
    for k, out_ref in enumerate(outs):
        at = lax.rem(y + k, len(outs)) * rows
        out_ref[...] = total_ref[pl.ds(pl.multiple_of(at, 8), rows), :]


def add_parts(place, parts):
    rows, width = parts[0].shape
    return call(
        add_kernel,
        "add_parts",
        [shape((rows // 4, width))] * 4,
        [pltpu.VMEM((rows, width), F32)],
        smem=1,
        flops=200_000,
        moved=1024 * 1024,
    )(place, *parts)


def cross_kernel(first_ref, second_ref, proj0_ref, proj1_ref, out_ref):
    width, rank = out_ref.shape
    tile = 512
    split = []
    for proj_ref in (proj0_ref, proj1_ref):
        proj = proj_ref[...]
        high = proj.astype(BF16)
        rest = proj - high.astype(F32)
        mid = rest.astype(BF16)
        low = (rest - mid.astype(F32)).astype(BF16)
        split.append((low, mid, high))

    def step(i, carry):
        at = pl.ds(pl.multiple_of(i * tile, tile), tile)
        total = None
        for block_ref, parts in zip((first_ref, second_ref), split):
            block = block_ref[:, at]
            for part in parts:
                term = product(block, part)
                total = term if total is None else total + term
        out_ref[at, :] = total
        return carry

    lax.fori_loop(0, width // tile, step, 0)


def cross(first, second, projs):
    width, rank = first.shape[1], projs[0].shape[1]
    return call(
        cross_kernel,
        "cross",
        shape((width, rank)),
        flops=4_000_000_000,
        moved=8 * 1024 * 1024,
    )(first, second, *projs)


def factor_kernel(place_ref, *refs):
    pieces, out_ref, packed_ref, work_ref = refs[:4], refs[4], refs[5], refs[6]
    side = len(pieces)
    rows = pieces[0].shape[1]
    y, x = place_ref[0], place_ref[1]
    for dx in range(side):
        for dy in range(side):
            source = lax.rem(x + side - dx, side) * side + lax.rem(y + side - dy, side)
            at = pl.ds(pl.multiple_of(source * rows, 8), rows)
            packed_ref[at, :] = pieces[dx][dy]
    size = work_ref.shape[0]
    steps = size // BLOCK
    place = 0
    for i in range(steps):
        for j in range(i + 1):
            piece = packed_ref[place * BLOCK : (place + 1) * BLOCK, :]
            work_ref[i * BLOCK : (i + 1) * BLOCK, j * BLOCK : (j + 1) * BLOCK] = piece
            place += 1
    for j in range(steps):
        lo, hi = j * BLOCK, (j + 1) * BLOCK
        inverse = eliminate(work_ref[lo:hi, lo:hi])
        out_ref[lo:hi, lo:hi] = inverse
        if j > 0:
            out_ref[lo:hi, :lo] = dot(inverse, work_ref[lo:hi, :lo])
        if j < steps - 1:
            out_ref[lo:hi, hi:] = jnp.zeros((BLOCK, size - hi), F32)
            low = dot(work_ref[hi:, lo:hi], inverse, turned=True)
            if j > 0:
                work_ref[hi:, :lo] -= dot(low, out_ref[lo:hi, :lo])
            work_ref[hi:, lo:hi] = -dot(low, inverse)
            work_ref[hi:, hi:] -= dot(low, low, turned=True)


def inverse_factor(place, pieces, rank):
    steps = rank // BLOCK
    packed = steps * (steps + 1) // 2 * BLOCK
    return call(
        factor_kernel,
        "inverse_factor",
        shape((rank, rank)),
        [pltpu.VMEM((packed, BLOCK), F32), pltpu.VMEM((rank, rank), F32)],
        smem=1,
        flops=24_000_000_000,
        moved=2 * 1024 * 1024,
    )(place, *pieces)


def finish_kernel(factor, place_ref, inverse_ref, *refs):
    pieces, blocks, projs = refs[:8], refs[8:10], refs[10:12]
    kept_refs, moved_refs, full_ref = refs[12:14], refs[14:16], refs[16]
    assemble(place_ref, pieces, full_ref)
    full = full_ref[...]
    wide = full.astype(F32)
    scaling = lax.rsqrt(jnp.mean(wide * wide, axis=0, keepdims=True) + root_eps)
    fresh = (wide * scaling).astype(BF16)
    inverse = inverse_ref[...]
    along = (((1,), (1,)), ((), ()))
    for i in range(2):
        basis = dot(projs[i][...], inverse, turned=True).astype(BF16)
        rounded = lax.dot_general(basis, full, along, preferred_element_type=F32)
        kept_refs[i][...] = (
            blocks[i][...].astype(F32) - (1.0 - momentum_decay) * rounded
        ).astype(BF16)
        turned = lax.dot_general(basis, fresh, along, preferred_element_type=F32)
        moved_refs[i][...] = (factor * turned).astype(BF16)


def finish(factor, place, inverse, pieces, blocks, projs):
    rows, width = blocks[0].shape
    out = call(
        lambda *refs: finish_kernel(factor, *refs),
        "finish",
        [shape((rows, width), BF16)] * 4,
        [pltpu.VMEM((width, inverse.shape[0]), BF16)],
        smem=1,
        flops=6_000_000_000,
        moved=10 * 1024 * 1024,
    )(place, inverse, *pieces, *blocks, *projs)
    return out[:2], out[2:]


def normalise_kernel(in_ref, out_ref):
    width = in_ref.shape[1]
    piece = 256

    def add(i, total):
        value = in_ref[0, pl.ds(i * piece, piece), :].astype(F32)
        return total + jnp.sum(value * value, axis=0, keepdims=True)

    total = lax.fori_loop(
        0, width // piece, add, jnp.zeros((1, in_ref.shape[2]), F32), unroll=True
    )
    scaling = lax.rsqrt(total / width + root_eps)

    def write(i, carry):
        at = pl.ds(i * piece, piece)
        out_ref[0, at, :] = (in_ref[0, at, :].astype(F32) * scaling).astype(BF16)
        return carry

    lax.fori_loop(0, width // piece, write, 0, unroll=True)


def normalise(x):
    spec = pl.BlockSpec((1,) + x.shape[1:], lambda s: (s, 0, 0))
    return pl.pallas_call(
        normalise_kernel,
        grid=(x.shape[0],),
        in_specs=[spec],
        out_specs=spec,
        out_shape=jax.ShapeDtypeStruct(x.shape, x.dtype),
        compiler_params=pltpu.CompilerParams(vmem_limit_bytes=32 * 1024 * 1024),
        cost_estimate=pl.CostEstimate(
            flops=20_000_000, bytes_accessed=2 * x.size * 2, transcendentals=0
        ),
        name="normalise",
    )(x)


def swap_core(x):
    return lax.ppermute(x, "core", [(0, 1), (1, 0)])


def shift(x, axis, k):
    n = lax.axis_size(axis)
    return lax.ppermute(x, axis, [(i, (i + k) % n) for i in range(n)])


def around(x, axis):
    far = {k: shift(x, axis, k) for k in (2, 1, 3)}
    return [x] + [far[k] for k in (1, 2, 3)]


def gather_plane(x):
    half = x.shape[1] // 2
    first = jnp.stack(around(x[:, :half], "x"))
    second = jnp.stack(around(x[:, half:], "y"))
    return around(first, "y") + around(second, "x")


def scatter_plane(x):
    chips = lax.axis_size(PLANE)
    parts = x.reshape((chips, x.shape[0] // chips) + x.shape[1:])
    return jnp.sum(lax.all_to_all(parts, PLANE, 0, 0, tiled=True), axis=0)


def local(momentum, gradient, qfactor, owner_of):
    groups = lax.axis_size("grp")
    chips = lax.axis_size(PLANE)
    homed, rows_local, width = momentum.shape
    owned, unused, rank = qfactor.shape
    total = owner_of.shape[0]
    group = lax.axis_index("grp")
    core = lax.axis_index("core")
    chip = lax.axis_index(PLANE)
    place = jnp.stack([lax.axis_index("y"), lax.axis_index("x")]).astype(jnp.int32)

    index = jnp.arange(total, dtype=jnp.int32)
    same = owner_of[:, None] == owner_of[None, :]
    earlier = index[None, :] < index[:, None]
    slot = jnp.sum((same & earlier).astype(jnp.int32), axis=1)
    hops = jnp.arange(groups, dtype=jnp.int32)
    after = (group + hops) % groups
    before = (group - hops + groups) % groups
    slots = jnp.arange(owned, dtype=jnp.int32)
    house = index // homed
    in_slot = (slot[:, None] == slots[None, :]) & (owner_of == group)[:, None]
    this_core = index % homed == core

    share = width // chips
    held = lax.dynamic_slice(qfactor, (0, chip * share, 0), (owned, share, rank))
    goes = (house[None, :] == after[:, None]) & this_core[None, :]
    goes = jnp.any(goes[:, :, None] & in_slot[None, :, :], axis=1)
    comes = (house == group) & this_core
    comes = jnp.any(comes[None, :] & (owner_of[None, :] == before[:, None]), axis=1)
    pieces = []
    for k in range(groups):
        piece = jnp.sum(jnp.where(goes[k][:, None, None], held, 0), axis=0, dtype=BF16)
        pieces.append(shift(piece, "grp", k) if k > 0 else piece)
    right = jnp.sum(
        jnp.where(comes[:, None, None], jnp.stack(pieces), 0), axis=0, dtype=BF16
    )
    pieces = gather_plane(right)

    blended = (momentum_decay * momentum.astype(F32) + gradient.astype(F32)).astype(BF16)
    keep = jnp.where(core == 0, blended[0], blended[1])
    give = jnp.where(core == 0, blended[1], blended[0])
    blocks = (keep, swap_core(give))

    projs, parts = project(place, *blocks, pieces)
    reduced = scatter_plane(cross(*blocks, projs))

    parts = [parts[0]] + [shift(parts[k], "x", k) for k in (1, 2, 3)]
    parts = add_parts(place, parts)
    parts = [parts[0]] + [shift(parts[k], "y", k) for k in (1, 2, 3)]
    part = (parts[0] + parts[1]) + (parts[2] + parts[3])
    inverse = inverse_factor(place, around(jnp.stack(around(part, "y")), "x"), rank)

    summed = dot(reduced, inverse, turned=True)
    rounded = summed.astype(BF16)

    half = share // 2
    lower, upper = rounded[:half], rounded[half:]
    stay = jnp.where(core == 0, lower, upper)
    other = swap_core(jnp.where(core == 0, upper, lower))
    first = jnp.where(core == 0, stay, other)
    second = jnp.where(core == 0, other, stay)
    theirs = (house == group)[None, :] & (owner_of[None, :] == after[:, None])
    theirs = jnp.any(theirs & (index % homed == 0)[None, :], axis=1)
    arrived = []
    for k in range(groups):
        piece = jnp.where(theirs[k : k + 1, None], first, second)
        arrived.append(shift(piece, "grp", k) if k > 0 else piece)
    taken = jnp.any(
        in_slot[:, :, None] & (house[:, None, None] == before[None, None, :]), axis=0
    )
    stacked = jnp.stack(arrived)
    filled = jnp.stack(
        [
            jnp.sum(jnp.where(taken[s][:, None, None], stacked, 0), axis=0, dtype=BF16)
            for s in range(owned)
        ]
    )
    new_qfactor = normalise(lax.all_gather(filled, ROWS, axis=1, tiled=True))

    factor = math.sqrt(2 * rows_local * chips * width / rank)
    kept, moved = finish(factor, place, inverse, gather_plane(rounded), blocks, projs)

    def home(stay, back):
        back = swap_core(back)
        return jnp.where(core == 0, jnp.stack([stay, back]), jnp.stack([back, stay]))

    return (home(*kept), home(*moved), new_qfactor)


def solution(mesh):
    fine = Mesh(mesh.devices.reshape(4, 4, 4, 2), ("grp", "y", "x", "core"))
    rows = P("grp", ROWS, None)
    return jax.shard_map(
        local,
        mesh=fine,
        in_specs=(rows, rows, P("grp", None, None), P()),
        out_specs=(rows, rows, P("grp", None, None)),
        check_vma=False,
    )
```

```python
import math

import jax
import jax.numpy as jnp
from jax import lax
from jax.experimental import pallas as pl
from jax.experimental.pallas import tpu as pltpu
from jax.sharding import Mesh
from jax.sharding import PartitionSpec as P

momentum_decay = 0.95
root_eps = 1e-06
HIGHEST = lax.Precision.HIGHEST
F32 = jnp.float32
BF16 = jnp.bfloat16
PLANE = ("y", "x")
ROWS = ("y", "x", "core")
BLOCK = 128


def eliminate(block):
    size = block.shape[0]
    lane = lax.broadcasted_iota(jnp.int32, (8, size), 1)
    sub = lax.broadcasted_iota(jnp.int32, (8, size), 0)
    count = size // 8

    def spread(tile, at):
        return jnp.broadcast_to(tile[:, at : at + 1], (8, size))

    def repeat(tile, at):
        return jnp.broadcast_to(tile[at : at + 1, :], (8, size))

    tiles = [block[8 * t : 8 * t + 8, :] for t in range(count)]
    done = []
    for t in range(count):
        base = 8 * t
        own = (lane >= base) & (lane < base + 8)
        columns = [spread(tiles[t], base + j) for j in range(8)]
        rows = jnp.where(own, jnp.where(lane == sub + base, 1.0, 0.0), tiles[t])
        result = None
        for k in range(8):
            here = sub == k
            inverse = 1.0 / repeat(columns[k], k)
            row = repeat(rows, k)
            value = row * jnp.sqrt(inverse)
            result = value if result is None else jnp.where(here, value, result)
            scaled = columns[k] * inverse
            for j in range(k + 1, 8):
                pivot = repeat(columns[j], k)
                columns[j] = jnp.where(here, pivot * inverse, columns[j] - scaled * pivot)
            rows = jnp.where(here, row * inverse, rows - scaled * row)
        done.append(jnp.where(lane <= sub + base, result, 0.0))
        solved = [repeat(rows, k) for k in range(8)]
        for u in range(t + 1, count):
            p = [spread(tiles[u], base + j) * solved[j] for j in range(8)]
            taken = ((p[0] + p[1]) + (p[2] + p[3])) + ((p[4] + p[5]) + (p[6] + p[7]))
            tiles[u] = jnp.where(own, 0.0, tiles[u]) - taken
    return jnp.concatenate(done, axis=0)


def dot(a, b, turned=False):
    return lax.dot_general(
        a,
        b,
        (((1,), (1 if turned else 0,)), ((), ())),
        precision=HIGHEST,
        preferred_element_type=F32,
    )


def product(a, b):
    return lax.dot_general(a, b, (((0,), (0,)), ((), ())), preferred_element_type=F32)


def call(kernel, name, out_shape, scratch=(), smem=0, flops=0, moved=0):
    def run(*args):
        specs = [
            pl.BlockSpec(memory_space=pltpu.SMEM if i < smem else pltpu.VMEM)
            for i in range(len(args))
        ]
        return pl.pallas_call(
            kernel,
            in_specs=specs,
            out_shape=out_shape,
            scratch_shapes=list(scratch),
            compiler_params=pltpu.CompilerParams(vmem_limit_bytes=24 * 1024 * 1024),
            cost_estimate=pl.CostEstimate(
                flops=flops, bytes_accessed=moved, transcendentals=0
            ),
            name=name,
        )(*args)

    return run


def shape(dims, dtype=F32):
    return jax.ShapeDtypeStruct(dims, dtype)


def assemble(place_ref, pieces, whole_ref):
    side = len(pieces) // 2
    share = pieces[0].shape[1]
    half = whole_ref.shape[1] // 2
    y, x = place_ref[0], place_ref[1]
    for i in range(side):
        for j in range(side):
            for part, (dy, dx) in enumerate(((i, j), (j, i))):
                chip = lax.rem(y + side - dy, side) * side + lax.rem(x + side - dx, side)
                at = pl.ds(pl.multiple_of(chip * share, share), share)
                piece = pieces[part * side + i]
                whole_ref[at, part * half : (part + 1) * half] = piece[j]


def project_kernel(place_ref, first_ref, second_ref, *refs):
    pieces, outs = refs[:8], refs[8:]
    proj_refs, part_refs, (right_ref, packed_ref) = outs[:2], outs[2:6], outs[6:]
    assemble(place_ref, pieces, right_ref)
    right = right_ref[...]
    rank = right.shape[1]
    projs = []
    for block_ref, proj_ref in zip((first_ref, second_ref), proj_refs):
        proj = jnp.dot(block_ref[...], right, preferred_element_type=F32)
        proj_ref[...] = proj
        projs.append(proj)
    place = 0
    for i in range(rank // BLOCK):
        lo, hi = i * BLOCK, (i + 1) * BLOCK
        wide = sum(
            lax.dot_general(
                proj[:, lo:hi],
                proj[:, :hi],
                (((0,), (0,)), ((), ())),
                precision=HIGHEST,
                preferred_element_type=F32,
            )
            for proj in projs
        )
        for j in range(i + 1):
            packed_ref[place * BLOCK : (place + 1) * BLOCK, :] = wide[
                :, j * BLOCK : (j + 1) * BLOCK
            ]
            place += 1
    x = place_ref[1]
    side = len(part_refs)
    rows = part_refs[0].shape[0]
    for k, part_ref in enumerate(part_refs):
        at = lax.rem(x + k, side) * rows
        part_ref[...] = packed_ref[pl.ds(pl.multiple_of(at, 8), rows), :]


def project(place, first, second, pieces):
    rows, width = first.shape
    rank = 2 * pieces[0].shape[2]
    steps = rank // BLOCK
    packed = steps * (steps + 1) // 2 * BLOCK
    out = call(
        project_kernel,
        "project",
        [shape((rows, rank))] * 2 + [shape((packed // 4, BLOCK))] * 4,
        [pltpu.VMEM((width, rank), BF16), pltpu.VMEM((packed, BLOCK), F32)],
        smem=1,
        flops=4_000_000_000,
        moved=6 * 1024 * 1024,
    )(place, first, second, *pieces)
    return out[:2], out[2:]


def add_kernel(place_ref, a_ref, b_ref, c_ref, d_ref, *refs):
    outs, total_ref = refs[:4], refs[4]
    total_ref[...] = (a_ref[...] + b_ref[...]) + (c_ref[...] + d_ref[...])
    y = place_ref[0]
    rows = outs[0].shape[0]
    for k, out_ref in enumerate(outs):
        at = lax.rem(y + k, len(outs)) * rows
        out_ref[...] = total_ref[pl.ds(pl.multiple_of(at, 8), rows), :]


def add_parts(place, parts):
    rows, width = parts[0].shape
    return call(
        add_kernel,
        "add_parts",
        [shape((rows // 4, width))] * 4,
        [pltpu.VMEM((rows, width), F32)],
        smem=1,
        flops=200_000,
        moved=1024 * 1024,
    )(place, *parts)


def cross_kernel(place_ref, *refs):
    blocks, proj_refs, outs, whole_ref = refs[:2], refs[2:4], refs[4:12], refs[12]
    width, rank = whole_ref.shape
    tile = 512
    split = []
    for proj_ref in proj_refs:
        proj = proj_ref[...]
        high = proj.astype(BF16)
        rest = proj - high.astype(F32)
        mid = rest.astype(BF16)
        low = (rest - mid.astype(F32)).astype(BF16)
        split.append((low, mid, high))

    def step(i, carry):
        at = pl.ds(pl.multiple_of(i * tile, tile), tile)
        total = None
        for block_ref, parts in zip(blocks, split):
            block = block_ref[:, at]
            for part in parts:
                term = product(block, part)
                total = term if total is None else total + term
        whole_ref[at, :] = total
        return carry

    lax.fori_loop(0, width // tile, step, 0)
    y, x = place_ref[0], place_ref[1]
    side, share, half = outs[0].shape
    for k in range(side):
        for i in range(side):
            for part, chip in enumerate(
                (i * side + lax.rem(x + k, side), lax.rem(y + k, side) * side + i)
            ):
                at = pl.ds(pl.multiple_of(chip * share, share), share)
                outs[part * side + k][i] = whole_ref[at, part * half : (part + 1) * half]


def cross(place, blocks, projs):
    width, rank = blocks[0].shape[1], projs[0].shape[1]
    share = width // 16
    return call(
        cross_kernel,
        "cross",
        [shape((4, share, rank // 2))] * 8,
        [pltpu.VMEM((width, rank), F32)],
        smem=1,
        flops=4_000_000_000,
        moved=8 * 1024 * 1024,
    )(place, *blocks, *projs)


def add_cross_kernel(place_ref, *refs):
    ins, outs, total_refs = refs[:8], refs[8:16], refs[16:18]
    for part in range(2):
        a, b, c, d = ins[4 * part : 4 * part + 4]
        total_refs[part][...] = (a[...] + b[...]) + (c[...] + d[...])
        for k in range(4):
            at = lax.rem(place_ref[part] + k, 4)
            outs[4 * part + k][...] = total_refs[part][at]


def add_cross(place, parts):
    side, share, half = parts[0].shape
    return call(
        add_cross_kernel,
        "add_cross",
        [shape((share, half))] * 8,
        [pltpu.VMEM((side, share, half), F32)] * 2,
        smem=1,
        flops=2_000_000,
        moved=5 * 1024 * 1024,
    )(place, *parts)


def close_kernel(*refs):
    ins, inverse_ref, out_ref = refs[:8], refs[8], refs[9]
    half = inverse_ref.shape[0] // 2
    total = None
    for part in range(2):
        a, b, c, d = ins[4 * part : 4 * part + 4]
        value = (a[...] + b[...]) + (c[...] + d[...])
        term = dot(value, inverse_ref[:, part * half : (part + 1) * half], turned=True)
        total = term if total is None else total + term
    out_ref[...] = total.astype(BF16)


def close(parts, inverse):
    share, half = parts[0].shape
    return call(
        close_kernel,
        "close",
        shape((share, 2 * half), BF16),
        flops=400_000_000,
        moved=3 * 1024 * 1024,
    )(*parts, inverse)


def factor_kernel(place_ref, *refs):
    pieces, out_ref, packed_ref, work_ref = refs[:4], refs[4], refs[5], refs[6]
    side = len(pieces)
    rows = pieces[0].shape[1]
    y, x = place_ref[0], place_ref[1]
    for dx in range(side):
        for dy in range(side):
            source = lax.rem(x + side - dx, side) * side + lax.rem(y + side - dy, side)
            at = pl.ds(pl.multiple_of(source * rows, 8), rows)
            packed_ref[at, :] = pieces[dx][dy]
    size = work_ref.shape[0]
    steps = size // BLOCK
    place = 0
    for i in range(steps):
        for j in range(i + 1):
            piece = packed_ref[place * BLOCK : (place + 1) * BLOCK, :]
            work_ref[i * BLOCK : (i + 1) * BLOCK, j * BLOCK : (j + 1) * BLOCK] = piece
            place += 1
    for j in range(steps):
        lo, hi = j * BLOCK, (j + 1) * BLOCK
        inverse = eliminate(work_ref[lo:hi, lo:hi])
        out_ref[lo:hi, lo:hi] = inverse
        if j > 0:
            out_ref[lo:hi, :lo] = dot(inverse, work_ref[lo:hi, :lo])
        if j < steps - 1:
            out_ref[lo:hi, hi:] = jnp.zeros((BLOCK, size - hi), F32)
            low = dot(work_ref[hi:, lo:hi], inverse, turned=True)
            if j > 0:
                work_ref[hi:, :lo] -= dot(low, out_ref[lo:hi, :lo])
            work_ref[hi:, lo:hi] = -dot(low, inverse)
            work_ref[hi:, hi:] -= dot(low, low, turned=True)


def inverse_factor(place, pieces, rank):
    steps = rank // BLOCK
    packed = steps * (steps + 1) // 2 * BLOCK
    return call(
        factor_kernel,
        "inverse_factor",
        shape((rank, rank)),
        [pltpu.VMEM((packed, BLOCK), F32), pltpu.VMEM((rank, rank), F32)],
        smem=1,
        flops=24_000_000_000,
        moved=2 * 1024 * 1024,
    )(place, *pieces)


def finish_kernel(factor, place_ref, inverse_ref, *refs):
    pieces, blocks, projs = refs[:8], refs[8:10], refs[10:12]
    kept_refs, moved_refs, full_ref = refs[12:14], refs[14:16], refs[16]
    assemble(place_ref, pieces, full_ref)
    full = full_ref[...]
    wide = full.astype(F32)
    scaling = lax.rsqrt(jnp.mean(wide * wide, axis=0, keepdims=True) + root_eps)
    fresh = (wide * scaling).astype(BF16)
    inverse = inverse_ref[...]
    along = (((1,), (1,)), ((), ()))
    for i in range(2):
        basis = dot(projs[i][...], inverse, turned=True).astype(BF16)
        rounded = lax.dot_general(basis, full, along, preferred_element_type=F32)
        kept_refs[i][...] = (
            blocks[i][...].astype(F32) - (1.0 - momentum_decay) * rounded
        ).astype(BF16)
        turned = lax.dot_general(basis, fresh, along, preferred_element_type=F32)
        moved_refs[i][...] = (factor * turned).astype(BF16)


def finish(factor, place, inverse, pieces, blocks, projs):
    rows, width = blocks[0].shape
    out = call(
        lambda *refs: finish_kernel(factor, *refs),
        "finish",
        [shape((rows, width), BF16)] * 4,
        [pltpu.VMEM((width, inverse.shape[0]), BF16)],
        smem=1,
        flops=6_000_000_000,
        moved=10 * 1024 * 1024,
    )(place, inverse, *pieces, *blocks, *projs)
    return out[:2], out[2:]


def normalise_kernel(in_ref, out_ref):
    width = in_ref.shape[1]
    piece = 256

    def add(i, total):
        value = in_ref[0, pl.ds(i * piece, piece), :].astype(F32)
        return total + jnp.sum(value * value, axis=0, keepdims=True)

    total = lax.fori_loop(
        0, width // piece, add, jnp.zeros((1, in_ref.shape[2]), F32), unroll=True
    )
    scaling = lax.rsqrt(total / width + root_eps)

    def write(i, carry):
        at = pl.ds(i * piece, piece)
        out_ref[0, at, :] = (in_ref[0, at, :].astype(F32) * scaling).astype(BF16)
        return carry

    lax.fori_loop(0, width // piece, write, 0, unroll=True)


def normalise(x):
    spec = pl.BlockSpec((1,) + x.shape[1:], lambda s: (s, 0, 0))
    return pl.pallas_call(
        normalise_kernel,
        grid=(x.shape[0],),
        in_specs=[spec],
        out_specs=spec,
        out_shape=jax.ShapeDtypeStruct(x.shape, x.dtype),
        compiler_params=pltpu.CompilerParams(vmem_limit_bytes=32 * 1024 * 1024),
        cost_estimate=pl.CostEstimate(
            flops=20_000_000, bytes_accessed=2 * x.size * 2, transcendentals=0
        ),
        name="normalise",
    )(x)


def swap_core(x):
    return lax.ppermute(x, "core", [(0, 1), (1, 0)])


def shift(x, axis, k):
    n = lax.axis_size(axis)
    return lax.ppermute(x, axis, [(i, (i + k) % n) for i in range(n)])


def around(x, axis):
    far = {k: shift(x, axis, k) for k in (2, 1, 3)}
    return [x] + [far[k] for k in (1, 2, 3)]


def gather_plane(x):
    half = x.shape[1] // 2
    first = jnp.stack(around(x[:, :half], "x"))
    second = jnp.stack(around(x[:, half:], "y"))
    return around(first, "y") + around(second, "x")


def spread_sum(terms, first, second):
    far = {}
    for k in (2, 1, 3):
        far[k] = shift(terms[k], first, k)
        far[k + 4] = shift(terms[k + 4], second, k)
    return [terms[0]] + [far[k] for k in (1, 2, 3)] + [terms[4]] + [far[k] for k in (5, 6, 7)]


def local(momentum, gradient, qfactor, owner_of):
    groups = lax.axis_size("grp")
    chips = lax.axis_size(PLANE)
    homed, rows_local, width = momentum.shape
    owned, unused, rank = qfactor.shape
    total = owner_of.shape[0]
    group = lax.axis_index("grp")
    core = lax.axis_index("core")
    chip = lax.axis_index(PLANE)
    place = jnp.stack([lax.axis_index("y"), lax.axis_index("x")]).astype(jnp.int32)

    index = jnp.arange(total, dtype=jnp.int32)
    same = owner_of[:, None] == owner_of[None, :]
    earlier = index[None, :] < index[:, None]
    slot = jnp.sum((same & earlier).astype(jnp.int32), axis=1)
    hops = jnp.arange(groups, dtype=jnp.int32)
    after = (group + hops) % groups
    before = (group - hops + groups) % groups
    slots = jnp.arange(owned, dtype=jnp.int32)
    house = index // homed
    in_slot = (slot[:, None] == slots[None, :]) & (owner_of == group)[:, None]
    this_core = index % homed == core

    share = width // chips
    held = lax.dynamic_slice(qfactor, (0, chip * share, 0), (owned, share, rank))
    goes = (house[None, :] == after[:, None]) & this_core[None, :]
    goes = jnp.any(goes[:, :, None] & in_slot[None, :, :], axis=1)
    comes = (house == group) & this_core
    comes = jnp.any(comes[None, :] & (owner_of[None, :] == before[:, None]), axis=1)
    pieces = []
    for k in range(groups):
        piece = jnp.sum(jnp.where(goes[k][:, None, None], held, 0), axis=0, dtype=BF16)
        pieces.append(shift(piece, "grp", k) if k > 0 else piece)
    right = jnp.sum(
        jnp.where(comes[:, None, None], jnp.stack(pieces), 0), axis=0, dtype=BF16
    )
    pieces = gather_plane(right)

    blended = (momentum_decay * momentum.astype(F32) + gradient.astype(F32)).astype(BF16)
    keep = jnp.where(core == 0, blended[0], blended[1])
    give = jnp.where(core == 0, blended[1], blended[0])
    blocks = (keep, swap_core(give))

    projs, parts = project(place, *blocks, pieces)

    parts = [parts[0]] + [shift(parts[k], "x", k) for k in (1, 2, 3)]
    parts, projs = lax.optimization_barrier((add_parts(place, parts), projs))
    terms = cross(place, blocks, projs)
    parts = [parts[0]] + [shift(parts[k], "y", k) for k in (1, 2, 3)]
    part = (parts[0] + parts[1]) + (parts[2] + parts[3])
    gram = jnp.stack(around(part, "y"))

    gram, terms = lax.optimization_barrier((gram, terms))
    grams, terms = lax.optimization_barrier((around(gram, "x"), terms))
    terms = spread_sum(terms, "x", "y")
    inverse = inverse_factor(place, grams, rank)
    inverse, terms = lax.optimization_barrier((inverse, terms))
    terms = spread_sum(add_cross(place, terms), "y", "x")
    rounded = close(terms, inverse)

    half = share // 2
    lower, upper = rounded[:half], rounded[half:]
    stay = jnp.where(core == 0, lower, upper)
    other = swap_core(jnp.where(core == 0, upper, lower))
    first = jnp.where(core == 0, stay, other)
    second = jnp.where(core == 0, other, stay)
    theirs = (house == group)[None, :] & (owner_of[None, :] == after[:, None])
    theirs = jnp.any(theirs & (index % homed == 0)[None, :], axis=1)
    arrived = []
    for k in range(groups):
        piece = jnp.where(theirs[k : k + 1, None], first, second)
        arrived.append(shift(piece, "grp", k) if k > 0 else piece)
    taken = jnp.any(
        in_slot[:, :, None] & (house[:, None, None] == before[None, None, :]), axis=0
    )
    stacked = jnp.stack(arrived)
    filled = jnp.stack(
        [
            jnp.sum(jnp.where(taken[s][:, None, None], stacked, 0), axis=0, dtype=BF16)
            for s in range(owned)
        ]
    )
    new_qfactor = normalise(lax.all_gather(filled, ROWS, axis=1, tiled=True))

    factor = math.sqrt(2 * rows_local * chips * width / rank)
    kept, moved = finish(factor, place, inverse, gather_plane(rounded), blocks, projs)

    def home(stay, back):
        back = swap_core(back)
        return jnp.where(core == 0, jnp.stack([stay, back]), jnp.stack([back, stay]))

    return (home(*kept), home(*moved), new_qfactor)


def solution(mesh):
    fine = Mesh(mesh.devices.reshape(4, 4, 4, 2), ("grp", "y", "x", "core"))
    rows = P("grp", ROWS, None)
    return jax.shard_map(
        local,
        mesh=fine,
        in_specs=(rows, rows, P("grp", None, None), P()),
        out_specs=(rows, rows, P("grp", None, None)),
        check_vma=False,
    )
```

```python
import math

import jax
import jax.numpy as jnp
from jax import lax
from jax.experimental import pallas as pl
from jax.experimental.pallas import tpu as pltpu
from jax.sharding import Mesh
from jax.sharding import PartitionSpec as P

momentum_decay = 0.95
root_eps = 1e-06
HIGHEST = lax.Precision.HIGHEST
F32 = jnp.float32
BF16 = jnp.bfloat16
PLANE = ("y", "x")
ROWS = ("y", "x", "core")
BLOCK = 128


def eliminate(block):
    size = block.shape[0]
    lane = lax.broadcasted_iota(jnp.int32, (8, size), 1)
    sub = lax.broadcasted_iota(jnp.int32, (8, size), 0)
    count = size // 8

    def spread(tile, at):
        return jnp.broadcast_to(tile[:, at : at + 1], (8, size))

    def repeat(tile, at):
        return jnp.broadcast_to(tile[at : at + 1, :], (8, size))

    tiles = [block[8 * t : 8 * t + 8, :] for t in range(count)]
    done = []
    for t in range(count):
        base = 8 * t
        own = (lane >= base) & (lane < base + 8)
        columns = [spread(tiles[t], base + j) for j in range(8)]
        rows = jnp.where(own, jnp.where(lane == sub + base, 1.0, 0.0), tiles[t])
        result = None
        for k in range(8):
            here = sub == k
            inverse = 1.0 / repeat(columns[k], k)
            row = repeat(rows, k)
            value = row * jnp.sqrt(inverse)
            result = value if result is None else jnp.where(here, value, result)
            scaled = columns[k] * inverse
            for j in range(k + 1, 8):
                pivot = repeat(columns[j], k)
                columns[j] = jnp.where(here, pivot * inverse, columns[j] - scaled * pivot)
            rows = jnp.where(here, row * inverse, rows - scaled * row)
        done.append(jnp.where(lane <= sub + base, result, 0.0))
        solved = [repeat(rows, k) for k in range(8)]
        for u in range(t + 1, count):
            p = [spread(tiles[u], base + j) * solved[j] for j in range(8)]
            taken = ((p[0] + p[1]) + (p[2] + p[3])) + ((p[4] + p[5]) + (p[6] + p[7]))
            tiles[u] = jnp.where(own, 0.0, tiles[u]) - taken
    return jnp.concatenate(done, axis=0)


def dot(a, b, turned=False):
    return lax.dot_general(
        a,
        b,
        (((1,), (1 if turned else 0,)), ((), ())),
        precision=HIGHEST,
        preferred_element_type=F32,
    )


def product(a, b):
    return lax.dot_general(a, b, (((0,), (0,)), ((), ())), preferred_element_type=F32)


def call(kernel, name, out_shape, scratch=(), smem=0, flops=0, moved=0):
    def run(*args):
        specs = [
            pl.BlockSpec(memory_space=pltpu.SMEM if i < smem else pltpu.VMEM)
            for i in range(len(args))
        ]
        return pl.pallas_call(
            kernel,
            in_specs=specs,
            out_shape=out_shape,
            scratch_shapes=list(scratch),
            compiler_params=pltpu.CompilerParams(vmem_limit_bytes=24 * 1024 * 1024),
            cost_estimate=pl.CostEstimate(
                flops=flops, bytes_accessed=moved, transcendentals=0
            ),
            name=name,
        )(*args)

    return run


def shape(dims, dtype=F32):
    return jax.ShapeDtypeStruct(dims, dtype)


def assemble(place_ref, pieces, whole_ref):
    side = len(pieces) // 2
    share = pieces[0].shape[1]
    half = whole_ref.shape[1] // 2
    y, x = place_ref[0], place_ref[1]
    for i in range(side):
        for j in range(side):
            for part, (dy, dx) in enumerate(((i, j), (j, i))):
                chip = lax.rem(y + side - dy, side) * side + lax.rem(x + side - dx, side)
                at = pl.ds(pl.multiple_of(chip * share, share), share)
                piece = pieces[part * side + i]
                whole_ref[at, part * half : (part + 1) * half] = piece[j]


def project_kernel(place_ref, first_ref, second_ref, *refs):
    pieces, outs = refs[:8], refs[8:]
    proj_refs, packed_ref, right_ref = outs[:2], outs[2], outs[3]
    assemble(place_ref, pieces, right_ref)
    right = right_ref[...]
    rank = right.shape[1]
    projs = []
    for block_ref, proj_ref in zip((first_ref, second_ref), proj_refs):
        proj = jnp.dot(block_ref[...], right, preferred_element_type=F32)
        proj_ref[...] = proj
        projs.append(proj)
    place = 0
    for i in range(rank // BLOCK):
        lo, hi = i * BLOCK, (i + 1) * BLOCK
        wide = sum(
            lax.dot_general(
                proj[:, lo:hi],
                proj[:, :hi],
                (((0,), (0,)), ((), ())),
                precision=HIGHEST,
                preferred_element_type=F32,
            )
            for proj in projs
        )
        for j in range(i + 1):
            packed_ref[place * BLOCK : (place + 1) * BLOCK, :] = wide[
                :, j * BLOCK : (j + 1) * BLOCK
            ]
            place += 1


def project(place, first, second, pieces):
    rows, width = first.shape
    rank = 2 * pieces[0].shape[2]
    steps = rank // BLOCK
    packed = steps * (steps + 1) // 2 * BLOCK
    out = call(
        project_kernel,
        "project",
        [shape((rows, rank))] * 2 + [shape((packed, BLOCK))],
        [pltpu.VMEM((width, rank), BF16)],
        smem=1,
        flops=4_000_000_000,
        moved=6 * 1024 * 1024,
    )(place, first, second, *pieces)
    return out[:2], out[2]


def cross_kernel(place_ref, *refs):
    blocks, proj_refs, outs, whole_ref = refs[:2], refs[2:4], refs[4:12], refs[12]
    width, rank = whole_ref.shape
    tile = 512
    split = []
    for proj_ref in proj_refs:
        proj = proj_ref[...]
        high = proj.astype(BF16)
        rest = proj - high.astype(F32)
        mid = rest.astype(BF16)
        low = (rest - mid.astype(F32)).astype(BF16)
        split.append((low, mid, high))

    def step(i, carry):
        at = pl.ds(pl.multiple_of(i * tile, tile), tile)
        total = None
        for block_ref, parts in zip(blocks, split):
            block = block_ref[:, at]
            for part in parts:
                term = product(block, part)
                total = term if total is None else total + term
        whole_ref[at, :] = total
        return carry

    lax.fori_loop(0, width // tile, step, 0)
    y, x = place_ref[0], place_ref[1]
    side, share, half = outs[0].shape
    for k in range(side):
        for i in range(side):
            for part, chip in enumerate(
                (i * side + lax.rem(x + k, side), lax.rem(y + k, side) * side + i)
            ):
                at = pl.ds(pl.multiple_of(chip * share, share), share)
                outs[part * side + k][i] = whole_ref[at, part * half : (part + 1) * half]


def cross(place, blocks, projs):
    width, rank = blocks[0].shape[1], projs[0].shape[1]
    share = width // 16
    return call(
        cross_kernel,
        "cross",
        [shape((4, share, rank // 2))] * 8,
        [pltpu.VMEM((width, rank), F32)],
        smem=1,
        flops=4_000_000_000,
        moved=8 * 1024 * 1024,
    )(place, *blocks, *projs)


def add_cross_kernel(place_ref, *refs):
    ins, outs, total_refs = refs[:8], refs[8:16], refs[16:18]
    for part in range(2):
        a, b, c, d = ins[4 * part : 4 * part + 4]
        total_refs[part][...] = (a[...] + b[...]) + (c[...] + d[...])
        for k in range(4):
            at = lax.rem(place_ref[part] + k, 4)
            outs[4 * part + k][...] = total_refs[part][at]


def add_cross(place, parts):
    side, share, half = parts[0].shape
    return call(
        add_cross_kernel,
        "add_cross",
        [shape((share, half))] * 8,
        [pltpu.VMEM((side, share, half), F32)] * 2,
        smem=1,
        flops=2_000_000,
        moved=5 * 1024 * 1024,
    )(place, *parts)


def close_kernel(*refs):
    ins, inverse_ref, out_ref = refs[:8], refs[8], refs[9]
    half = inverse_ref.shape[0] // 2
    total = None
    for part in range(2):
        a, b, c, d = ins[4 * part : 4 * part + 4]
        value = (a[...] + b[...]) + (c[...] + d[...])
        term = dot(value, inverse_ref[:, part * half : (part + 1) * half], turned=True)
        total = term if total is None else total + term
    out_ref[...] = total.astype(BF16)


def close(parts, inverse):
    share, half = parts[0].shape
    return call(
        close_kernel,
        "close",
        shape((share, 2 * half), BF16),
        flops=400_000_000,
        moved=3 * 1024 * 1024,
    )(*parts, inverse)


def factor_kernel(packed_ref, out_ref, work_ref):
    size = work_ref.shape[0]
    steps = size // BLOCK
    place = 0
    for i in range(steps):
        for j in range(i + 1):
            piece = packed_ref[place * BLOCK : (place + 1) * BLOCK, :]
            work_ref[i * BLOCK : (i + 1) * BLOCK, j * BLOCK : (j + 1) * BLOCK] = piece
            place += 1
    for j in range(steps):
        lo, hi = j * BLOCK, (j + 1) * BLOCK
        inverse = eliminate(work_ref[lo:hi, lo:hi])
        out_ref[lo:hi, lo:hi] = inverse
        if j > 0:
            out_ref[lo:hi, :lo] = dot(inverse, work_ref[lo:hi, :lo])
        if j < steps - 1:
            out_ref[lo:hi, hi:] = jnp.zeros((BLOCK, size - hi), F32)
            low = dot(work_ref[hi:, lo:hi], inverse, turned=True)
            if j > 0:
                work_ref[hi:, :lo] -= dot(low, out_ref[lo:hi, :lo])
            work_ref[hi:, lo:hi] = -dot(low, inverse)
            work_ref[hi:, hi:] -= dot(low, low, turned=True)


def inverse_factor(packed, rank):
    return call(
        factor_kernel,
        "inverse_factor",
        shape((rank, rank)),
        [pltpu.VMEM((rank, rank), F32)],
        flops=24_000_000_000,
        moved=2 * 1024 * 1024,
    )(packed)


def finish_kernel(factor, place_ref, inverse_ref, *refs):
    pieces, blocks, projs = refs[:8], refs[8:10], refs[10:12]
    kept_refs, moved_refs, full_ref = refs[12:14], refs[14:16], refs[16]
    assemble(place_ref, pieces, full_ref)
    full = full_ref[...]
    wide = full.astype(F32)
    scaling = lax.rsqrt(jnp.mean(wide * wide, axis=0, keepdims=True) + root_eps)
    fresh = (wide * scaling).astype(BF16)
    inverse = inverse_ref[...]
    along = (((1,), (1,)), ((), ()))
    for i in range(2):
        basis = dot(projs[i][...], inverse, turned=True).astype(BF16)
        rounded = lax.dot_general(basis, full, along, preferred_element_type=F32)
        kept_refs[i][...] = (
            blocks[i][...].astype(F32) - (1.0 - momentum_decay) * rounded
        ).astype(BF16)
        turned = lax.dot_general(basis, fresh, along, preferred_element_type=F32)
        moved_refs[i][...] = (factor * turned).astype(BF16)


def finish(factor, place, inverse, pieces, blocks, projs):
    rows, width = blocks[0].shape
    out = call(
        lambda *refs: finish_kernel(factor, *refs),
        "finish",
        [shape((rows, width), BF16)] * 4,
        [pltpu.VMEM((width, inverse.shape[0]), BF16)],
        smem=1,
        flops=6_000_000_000,
        moved=10 * 1024 * 1024,
    )(place, inverse, *pieces, *blocks, *projs)
    return out[:2], out[2:]


def normalise_kernel(in_ref, out_ref):
    width = in_ref.shape[1]
    piece = 256

    def add(i, total):
        value = in_ref[0, pl.ds(i * piece, piece), :].astype(F32)
        return total + jnp.sum(value * value, axis=0, keepdims=True)

    total = lax.fori_loop(
        0, width // piece, add, jnp.zeros((1, in_ref.shape[2]), F32), unroll=True
    )
    scaling = lax.rsqrt(total / width + root_eps)

    def write(i, carry):
        at = pl.ds(i * piece, piece)
        out_ref[0, at, :] = (in_ref[0, at, :].astype(F32) * scaling).astype(BF16)
        return carry

    lax.fori_loop(0, width // piece, write, 0, unroll=True)


def normalise(x):
    spec = pl.BlockSpec((1,) + x.shape[1:], lambda s: (s, 0, 0))
    return pl.pallas_call(
        normalise_kernel,
        grid=(x.shape[0],),
        in_specs=[spec],
        out_specs=spec,
        out_shape=jax.ShapeDtypeStruct(x.shape, x.dtype),
        compiler_params=pltpu.CompilerParams(vmem_limit_bytes=60 * 1024 * 1024),
        cost_estimate=pl.CostEstimate(
            flops=20_000_000, bytes_accessed=2 * x.size * 2, transcendentals=0
        ),
        name="normalise",
    )(x)


def swap_core(x):
    return lax.ppermute(x, "core", [(0, 1), (1, 0)])


def shift(x, axis, k):
    n = lax.axis_size(axis)
    return lax.ppermute(x, axis, [(i, (i + k) % n) for i in range(n)])


def around(x, axis):
    far = {k: shift(x, axis, k) for k in (2, 1, 3)}
    return [x] + [far[k] for k in (1, 2, 3)]


def gather_plane(x):
    half = x.shape[1] // 2
    first = jnp.stack(around(x[:, :half], "x"))
    second = jnp.stack(around(x[:, half:], "y"))
    first, second = lax.optimization_barrier((first, second))
    return around(first, "y") + around(second, "x")


def spread_sum(terms, first, second):
    far = {}
    for k in (2, 1, 3):
        far[k] = shift(terms[k], first, k)
        far[k + 4] = shift(terms[k + 4], second, k)
    return [terms[0]] + [far[k] for k in (1, 2, 3)] + [terms[4]] + [far[k] for k in (5, 6, 7)]


def local(momentum, gradient, qfactor, owner_of):
    groups = lax.axis_size("grp")
    chips = lax.axis_size(PLANE)
    homed, rows_local, width = momentum.shape
    owned, unused, rank = qfactor.shape
    total = owner_of.shape[0]
    group = lax.axis_index("grp")
    core = lax.axis_index("core")
    chip = lax.axis_index(PLANE)
    place = jnp.stack([lax.axis_index("y"), lax.axis_index("x")]).astype(jnp.int32)

    index = jnp.arange(total, dtype=jnp.int32)
    same = owner_of[:, None] == owner_of[None, :]
    earlier = index[None, :] < index[:, None]
    slot = jnp.sum((same & earlier).astype(jnp.int32), axis=1)
    hops = jnp.arange(groups, dtype=jnp.int32)
    after = (group + hops) % groups
    before = (group - hops + groups) % groups
    slots = jnp.arange(owned, dtype=jnp.int32)
    house = index // homed
    in_slot = (slot[:, None] == slots[None, :]) & (owner_of == group)[:, None]
    this_core = index % homed == core

    share = width // chips
    held = lax.dynamic_slice(qfactor, (0, chip * share, 0), (owned, share, rank))
    goes = (house[None, :] == after[:, None]) & this_core[None, :]
    goes = jnp.any(goes[:, :, None] & in_slot[None, :, :], axis=1)
    comes = (house == group) & this_core
    comes = jnp.any(comes[None, :] & (owner_of[None, :] == before[:, None]), axis=1)
    pieces = []
    for k in range(groups):
        piece = jnp.sum(jnp.where(goes[k][:, None, None], held, 0), axis=0, dtype=BF16)
        pieces.append(shift(piece, "grp", k) if k > 0 else piece)
    right = jnp.sum(
        jnp.where(comes[:, None, None], jnp.stack(pieces), 0), axis=0, dtype=BF16
    )
    pieces = gather_plane(right)

    blended = (momentum_decay * momentum.astype(F32) + gradient.astype(F32)).astype(BF16)
    keep = jnp.where(core == 0, blended[0], blended[1])
    give = jnp.where(core == 0, blended[1], blended[0])
    blocks = (keep, swap_core(give))

    projs, packed = project(place, *blocks, pieces)

    parts = packed.reshape(chips, packed.shape[0] // chips, BLOCK)
    part = jnp.sum(lax.all_to_all(parts, PLANE, 0, 0, tiled=True), axis=0)
    terms = cross(place, blocks, projs)
    part, terms = lax.optimization_barrier((part, terms))
    many = jnp.broadcast_to(part[None], (chips,) + part.shape)
    gram = lax.all_to_all(many, PLANE, 0, 0, tiled=True)
    inverse = inverse_factor(gram.reshape(-1, BLOCK), rank)
    terms = spread_sum(terms, "x", "y")
    inverse, terms = lax.optimization_barrier((inverse, terms))
    terms = spread_sum(add_cross(place, terms), "y", "x")
    rounded = close(terms, inverse)

    half = share // 2
    lower, upper = rounded[:half], rounded[half:]
    stay = jnp.where(core == 0, lower, upper)
    other = swap_core(jnp.where(core == 0, upper, lower))
    first = jnp.where(core == 0, stay, other)
    second = jnp.where(core == 0, other, stay)
    theirs = (house == group)[None, :] & (owner_of[None, :] == after[:, None])
    theirs = jnp.any(theirs & (index % homed == 0)[None, :], axis=1)
    arrived = []
    for k in range(groups):
        piece = jnp.where(theirs[k : k + 1, None], first, second)
        arrived.append(shift(piece, "grp", k) if k > 0 else piece)
    taken = jnp.any(
        in_slot[:, :, None] & (house[:, None, None] == before[None, None, :]), axis=0
    )
    stacked = jnp.stack(arrived)
    filled = jnp.stack(
        [
            jnp.sum(jnp.where(taken[s][:, None, None], stacked, 0), axis=0, dtype=BF16)
            for s in range(owned)
        ]
    )
    new_qfactor = normalise(lax.all_gather(filled, ROWS, axis=1, tiled=True))

    factor = math.sqrt(2 * rows_local * chips * width / rank)
    kept, moved = finish(factor, place, inverse, gather_plane(rounded), blocks, projs)

    def home(stay, back):
        back = swap_core(back)
        return jnp.where(core == 0, jnp.stack([stay, back]), jnp.stack([back, stay]))

    return (home(*kept), home(*moved), new_qfactor)


def solution(mesh):
    fine = Mesh(mesh.devices.reshape(4, 4, 4, 2), ("grp", "y", "x", "core"))
    rows = P("grp", ROWS, None)
    return jax.shard_map(
        local,
        mesh=fine,
        in_specs=(rows, rows, P("grp", None, None), P()),
        out_specs=(rows, rows, P("grp", None, None)),
        check_vma=False,
    )
```

```python
import math

import jax
import jax.numpy as jnp
from jax import lax
from jax.experimental import pallas as pl
from jax.experimental.pallas import tpu as pltpu
from jax.sharding import Mesh
from jax.sharding import PartitionSpec as P

momentum_decay = 0.95
root_eps = 1e-06
HIGHEST = lax.Precision.HIGHEST
F32 = jnp.float32
BF16 = jnp.bfloat16
PLANE = ("y", "x")
ROWS = ("y", "x", "core")
BLOCK = 128


def eliminate(block):
    size = block.shape[0]
    lane = lax.broadcasted_iota(jnp.int32, (8, size), 1)
    sub = lax.broadcasted_iota(jnp.int32, (8, size), 0)
    count = size // 8

    def spread(tile, at):
        return jnp.broadcast_to(tile[:, at : at + 1], (8, size))

    def repeat(tile, at):
        return jnp.broadcast_to(tile[at : at + 1, :], (8, size))

    tiles = [block[8 * t : 8 * t + 8, :] for t in range(count)]
    done = []
    for t in range(count):
        base = 8 * t
        own = (lane >= base) & (lane < base + 8)
        columns = [spread(tiles[t], base + j) for j in range(8)]
        rows = jnp.where(own, jnp.where(lane == sub + base, 1.0, 0.0), tiles[t])
        result = None
        for k in range(8):
            here = sub == k
            inverse = 1.0 / repeat(columns[k], k)
            row = repeat(rows, k)
            value = row * jnp.sqrt(inverse)
            result = value if result is None else jnp.where(here, value, result)
            scaled = columns[k] * inverse
            for j in range(k + 1, 8):
                pivot = repeat(columns[j], k)
                columns[j] = jnp.where(here, pivot * inverse, columns[j] - scaled * pivot)
            rows = jnp.where(here, row * inverse, rows - scaled * row)
        done.append(jnp.where(lane <= sub + base, result, 0.0))
        solved = [repeat(rows, k) for k in range(8)]
        for u in range(t + 1, count):
            p = [spread(tiles[u], base + j) * solved[j] for j in range(8)]
            taken = ((p[0] + p[1]) + (p[2] + p[3])) + ((p[4] + p[5]) + (p[6] + p[7]))
            tiles[u] = jnp.where(own, 0.0, tiles[u]) - taken
    return jnp.concatenate(done, axis=0)


def dot(a, b, turned=False):
    return lax.dot_general(
        a,
        b,
        (((1,), (1 if turned else 0,)), ((), ())),
        precision=HIGHEST,
        preferred_element_type=F32,
    )


def product(a, b):
    return lax.dot_general(a, b, (((0,), (0,)), ((), ())), preferred_element_type=F32)


def call(kernel, name, out_shape, scratch=(), smem=0, flops=0, moved=0):
    def run(*args):
        specs = [
            pl.BlockSpec(memory_space=pltpu.SMEM if i < smem else pltpu.VMEM)
            for i in range(len(args))
        ]
        return pl.pallas_call(
            kernel,
            in_specs=specs,
            out_shape=out_shape,
            scratch_shapes=list(scratch),
            compiler_params=pltpu.CompilerParams(vmem_limit_bytes=24 * 1024 * 1024),
            cost_estimate=pl.CostEstimate(
                flops=flops, bytes_accessed=moved, transcendentals=0
            ),
            name=name,
        )(*args)

    return run


def shape(dims, dtype=F32):
    return jax.ShapeDtypeStruct(dims, dtype)


def assemble(place_ref, pieces, whole_ref):
    side = len(pieces) // 2
    share = pieces[0].shape[1]
    half = whole_ref.shape[1] // 2
    y, x = place_ref[0], place_ref[1]
    for i in range(side):
        for j in range(side):
            for part, (dy, dx) in enumerate(((i, j), (j, i))):
                chip = lax.rem(y + side - dy, side) * side + lax.rem(x + side - dx, side)
                at = pl.ds(pl.multiple_of(chip * share, share), share)
                piece = pieces[part * side + i]
                whole_ref[at, part * half : (part + 1) * half] = piece[j]


def project_kernel(place_ref, first_ref, second_ref, *refs):
    pieces, outs = refs[:8], refs[8:]
    proj_refs, packed_ref, right_ref = outs[:2], outs[2], outs[3]
    assemble(place_ref, pieces, right_ref)
    right = right_ref[...]
    rank = right.shape[1]
    projs = []
    for block_ref, proj_ref in zip((first_ref, second_ref), proj_refs):
        proj = jnp.dot(block_ref[...], right, preferred_element_type=F32)
        proj_ref[...] = proj
        projs.append(proj)
    place = 0
    for i in range(rank // BLOCK):
        lo, hi = i * BLOCK, (i + 1) * BLOCK
        wide = sum(
            lax.dot_general(
                proj[:, lo:hi],
                proj[:, :hi],
                (((0,), (0,)), ((), ())),
                precision=HIGHEST,
                preferred_element_type=F32,
            )
            for proj in projs
        )
        for j in range(i + 1):
            packed_ref[place * BLOCK : (place + 1) * BLOCK, :] = wide[
                :, j * BLOCK : (j + 1) * BLOCK
            ]
            place += 1


def project(place, first, second, pieces):
    rows, width = first.shape
    rank = 2 * pieces[0].shape[2]
    steps = rank // BLOCK
    packed = steps * (steps + 1) // 2 * BLOCK
    out = call(
        project_kernel,
        "project",
        [shape((rows, rank))] * 2 + [shape((packed, BLOCK))],
        [pltpu.VMEM((width, rank), BF16)],
        smem=1,
        flops=4_000_000_000,
        moved=6 * 1024 * 1024,
    )(place, first, second, *pieces)
    return out[:2], out[2]


def partial_kernel(inverse_ref, *refs):
    blocks, projs, bases, out_ref = refs[:2], refs[2:4], refs[4:6], refs[6]
    chips, share, rank = out_ref.shape
    tile = 4
    inverse = inverse_ref[...]
    values = []
    for proj_ref, basis_ref in zip(projs, bases):
        basis = dot(proj_ref[...], inverse, turned=True).astype(BF16)
        basis_ref[...] = basis
        values.append(basis)

    def step(i, carry):
        at = pl.ds(pl.multiple_of(i * tile * share, tile * share), tile * share)
        total = sum(product(ref[:, at], basis) for ref, basis in zip(blocks, values))
        out_ref[pl.ds(i * tile, tile)] = total.astype(BF16).reshape(tile, share, rank)
        return carry

    lax.fori_loop(0, chips // tile, step, 0)


def partial(inverse, blocks, projs):
    rows, rank = projs[0].shape
    width = blocks[0].shape[1]
    out = call(
        partial_kernel,
        "partial",
        [shape((rows, rank), BF16)] * 2 + [shape((16, width // 16, rank), BF16)],
        flops=3_000_000_000,
        moved=7 * 1024 * 1024,
    )(inverse, *blocks, *projs)
    return out[:2], out[2]


def factor_kernel(packed_ref, out_ref, work_ref):
    size = work_ref.shape[0]
    steps = size // BLOCK
    place = 0
    for i in range(steps):
        for j in range(i + 1):
            piece = packed_ref[place * BLOCK : (place + 1) * BLOCK, :]
            work_ref[i * BLOCK : (i + 1) * BLOCK, j * BLOCK : (j + 1) * BLOCK] = piece
            place += 1
    for j in range(steps):
        lo, hi = j * BLOCK, (j + 1) * BLOCK
        inverse = eliminate(work_ref[lo:hi, lo:hi])
        out_ref[lo:hi, lo:hi] = inverse
        if j > 0:
            out_ref[lo:hi, :lo] = dot(inverse, work_ref[lo:hi, :lo])
        if j < steps - 1:
            out_ref[lo:hi, hi:] = jnp.zeros((BLOCK, size - hi), F32)
            low = dot(work_ref[hi:, lo:hi], inverse, turned=True)
            if j > 0:
                work_ref[hi:, :lo] -= dot(low, out_ref[lo:hi, :lo])
            work_ref[hi:, lo:hi] = -dot(low, inverse)
            work_ref[hi:, hi:] -= dot(low, low, turned=True)


def inverse_factor(packed, rank):
    return call(
        factor_kernel,
        "inverse_factor",
        shape((rank, rank)),
        [pltpu.VMEM((rank, rank), F32)],
        flops=24_000_000_000,
        moved=2 * 1024 * 1024,
    )(packed)


def scale_rows(read, write, rows, rank):
    step = 32

    def add(i, total):
        value = read(i * step, step).astype(F32)
        return total + jnp.sum(value * value, axis=0, keepdims=True)

    total = lax.fori_loop(0, rows // step, add, jnp.zeros((1, rank), F32), unroll=4)
    scaling = lax.rsqrt(total / rows + root_eps)

    def store(i, carry):
        write(i * step, (read(i * step, step).astype(F32) * scaling).astype(BF16))
        return carry

    lax.fori_loop(0, rows // step, store, 0, unroll=4)


def interleave(low_ref, high_ref, out_ref):
    chips, rows, rank = low_ref.shape
    for chip in range(chips):
        at = 2 * chip * rows
        out_ref[at : at + rows, :] = low_ref[chip]
        out_ref[at + rows : at + 2 * rows, :] = high_ref[chip]


def split_kernel(place_ref, picks_ref, *refs):
    pieces, both_ref, sends, whole_ref = refs[:8], refs[8], refs[9:11], refs[11]
    assemble(place_ref, pieces, whole_ref)
    homed, chips, rows, rank = both_ref.shape
    for chip in range(chips):
        for h in range(homed):
            at = (chip * homed + h) * rows
            both_ref[h, chip] = whole_ref[at : at + rows, :]
    for send_ref, k in zip(sends, (1, 3)):
        send_ref[...] = both_ref[1 - picks_ref[k]]


def split(place, picks, pieces, homed):
    share, half = pieces[0].shape[1:]
    dims = (16, share // homed, 2 * half)
    return call(
        split_kernel,
        "split",
        [shape((homed,) + dims, BF16)] + [shape(dims, BF16)] * 2,
        [pltpu.VMEM((16 * share, 2 * half), BF16)],
        smem=2,
        flops=1_000_000,
        moved=6 * 1024 * 1024,
    )(place, picks, *pieces)


def scale_kernel(place_ref, both_ref, facing_ref, full_ref, fresh_ref):
    core = place_ref[2]
    for first in range(2):

        @pl.when(core == first)
        def _():
            refs = (both_ref.at[first], facing_ref.at[first])
            interleave(refs[first], refs[1 - first], full_ref)

    rows, rank = full_ref.shape

    def read(at, size):
        return full_ref[pl.ds(pl.multiple_of(at, size), size), :]

    def write(at, value):
        size = value.shape[0]
        fresh_ref[pl.ds(pl.multiple_of(at, size), size), :] = value

    scale_rows(read, write, rows, rank)


def scale(place, both, facing):
    homed, chips, rows, rank = both.shape
    return call(
        scale_kernel,
        "scale",
        [shape((2 * chips * rows, rank), BF16)] * 2,
        smem=1,
        flops=10_000_000,
        moved=8 * 1024 * 1024,
    )(place, both, facing)


def finish_kernel(factor, place_ref, full_ref, fresh_ref, *refs):
    blocks, bases, wholes, gives = refs[:2], refs[2:4], refs[4:6], refs[6:8]
    stays, sems = refs[8:10], refs[10]
    full, fresh = full_ref[...], fresh_ref[...]
    along = (((1,), (1,)), ((), ()))
    copies = []
    for i in (1, 0):
        outs = gives if i == 1 else stays
        basis = bases[i][...]
        rounded = lax.dot_general(basis, full, along, preferred_element_type=F32)
        outs[0][...] = (
            blocks[i][...].astype(F32) - (1.0 - momentum_decay) * rounded
        ).astype(BF16)
        turned = lax.dot_general(basis, fresh, along, preferred_element_type=F32)
        outs[1][...] = (factor * turned).astype(BF16)
    for i in range(2):
        copy = pltpu.make_async_copy(stays[i], wholes[i].at[place_ref[2]], sems.at[i])
        copy.start()
        copies.append(copy)
    for copy in copies:
        copy.wait()


def finish(factor, place, full, fresh, blocks, bases):
    rows, width = blocks[0].shape
    vmem = pl.BlockSpec(memory_space=pltpu.VMEM)
    anywhere = pl.BlockSpec(memory_space=pl.ANY)
    out = pl.pallas_call(
        lambda *refs: finish_kernel(factor, *refs),
        in_specs=[pl.BlockSpec(memory_space=pltpu.SMEM)] + [vmem] * 6,
        out_specs=[anywhere] * 2 + [vmem] * 2,
        out_shape=[shape((2, rows, width), BF16)] * 2 + [shape((rows, width), BF16)] * 2,
        scratch_shapes=[pltpu.VMEM((rows, width), BF16)] * 2
        + [pltpu.SemaphoreType.DMA((2,))],
        compiler_params=pltpu.CompilerParams(vmem_limit_bytes=24 * 1024 * 1024),
        cost_estimate=pl.CostEstimate(
            flops=6_000_000_000, bytes_accessed=10 * 1024 * 1024, transcendentals=0
        ),
        name="finish",
    )(place, full, fresh, *blocks, *bases)
    return out[:2], out[2:]


def put_rows(whole, place, back):
    def kernel(place_ref, unused, back_ref, out_ref, sems):
        copy = pltpu.make_async_copy(back_ref, out_ref.at[1 - place_ref[2]], sems.at[0])
        copy.start()
        copy.wait()

    return put(kernel, "put_rows", whole, place, (back,))


def put(kernel, name, whole, meta, values, scratch=()):
    anywhere = pl.BlockSpec(memory_space=pl.ANY)
    smem = pl.BlockSpec(memory_space=pltpu.SMEM)
    return pl.pallas_call(
        kernel,
        in_specs=[smem, anywhere]
        + [pl.BlockSpec(memory_space=pltpu.VMEM)] * len(values),
        out_specs=anywhere,
        out_shape=shape(whole.shape, whole.dtype),
        input_output_aliases={1: 0},
        scratch_shapes=list(scratch) + [pltpu.SemaphoreType.DMA((2,))],
        compiler_params=pltpu.CompilerParams(vmem_limit_bytes=16 * 1024 * 1024),
        cost_estimate=pl.CostEstimate(
            flops=0, bytes_accessed=4 * 1024 * 1024, transcendentals=0
        ),
        name=name,
    )(meta, whole, *values)


def put_expert(k, whole, meta, mine, other):
    chips, rows, rank = mine.shape[-3:]

    def kernel(meta_ref, unused, mine_ref, other_ref, out_ref, new_ref, sems):
        parity = meta_ref[k, 2]
        for first in range(2):

            @pl.when((meta_ref[k, 0] == 1) & (meta_ref[k, 3] == first))
            def _():
                refs = (mine_ref, other_ref)
                if len(mine.shape) == 4:
                    refs = (mine_ref.at[parity], other_ref.at[parity])
                interleave(refs[first], refs[1 - first], new_ref)

        @pl.when(meta_ref[k, 0] == 1)
        def _():
            def read(at, size):
                return new_ref[pl.ds(pl.multiple_of(at, size), size), :]

            def write(at, value):
                size = value.shape[0]
                new_ref[pl.ds(pl.multiple_of(at, size), size), :] = value

            scale_rows(read, write, 2 * chips * rows, rank)
            copy = pltpu.make_async_copy(new_ref, out_ref.at[meta_ref[k, 1]], sems.at[0])
            copy.start()
            copy.wait()

    scratch = (pltpu.VMEM((2 * chips * rows, rank), BF16),)
    return put(kernel, "put_expert", whole, meta, (mine, other), scratch)


def blank(place, dims):
    def kernel(unused, out_ref, zero_ref, sems):
        zero_ref[...] = jnp.zeros_like(zero_ref)
        copies = [
            pltpu.make_async_copy(zero_ref, out_ref.at[i], sems.at[i])
            for i in range(dims[0])
        ]
        for copy in copies:
            copy.start()
        for copy in copies:
            copy.wait()

    return pl.pallas_call(
        kernel,
        in_specs=[pl.BlockSpec(memory_space=pltpu.SMEM)],
        out_specs=pl.BlockSpec(memory_space=pl.ANY),
        out_shape=shape(dims, BF16),
        scratch_shapes=[pltpu.VMEM(dims[1:], BF16), pltpu.SemaphoreType.DMA((dims[0],))],
        compiler_params=pltpu.CompilerParams(vmem_limit_bytes=16 * 1024 * 1024),
        cost_estimate=pl.CostEstimate(
            flops=0, bytes_accessed=8 * 1024 * 1024, transcendentals=0
        ),
        name="blank",
    )(place)


def swap_core(x):
    return lax.ppermute(x, "core", [(0, 1), (1, 0)])


def shift(x, axis, k):
    n = lax.axis_size(axis)
    return lax.ppermute(x, axis, [(i, (i + k) % n) for i in range(n)])


def around(x, axis):
    far = {k: shift(x, axis, k) for k in (2, 1, 3)}
    return [x] + [far[k] for k in (1, 2, 3)]


def gather_plane(x, beside=()):
    half = x.shape[1] // 2
    first = jnp.stack(around(x[:, :half], "x"))
    second = jnp.stack(around(x[:, half:], "y"))
    first, second, beside = lax.optimization_barrier((first, second, beside))
    return around(first, "y") + around(second, "x"), beside


def local(momentum, gradient, qfactor, owner_of):
    groups = lax.axis_size("grp")
    chips = lax.axis_size(PLANE)
    homed, rows_local, width = momentum.shape
    owned, unused, rank = qfactor.shape
    total = owner_of.shape[0]
    group = lax.axis_index("grp")
    core = lax.axis_index("core")
    chip = lax.axis_index(PLANE)
    place = jnp.stack([lax.axis_index("y"), lax.axis_index("x"), core]).astype(jnp.int32)

    index = jnp.arange(total, dtype=jnp.int32)
    same = owner_of[:, None] == owner_of[None, :]
    earlier = index[None, :] < index[:, None]
    slot = jnp.sum((same & earlier).astype(jnp.int32), axis=1)
    hops = jnp.arange(groups, dtype=jnp.int32)
    after = (group + hops) % groups
    before = (group - hops + groups) % groups
    slots = jnp.arange(owned, dtype=jnp.int32)
    house = index // homed
    in_slot = (slot[:, None] == slots[None, :]) & (owner_of == group)[:, None]
    this_core = index % homed == core

    share = width // chips
    held = lax.dynamic_slice(qfactor, (0, chip * share, 0), (owned, share, rank))
    goes = (house[None, :] == after[:, None]) & this_core[None, :]
    goes = jnp.any(goes[:, :, None] & in_slot[None, :, :], axis=1)
    comes = (house == group) & this_core
    comes = jnp.any(comes[None, :] & (owner_of[None, :] == before[:, None]), axis=1)
    pieces = []
    for k in range(groups):
        piece = jnp.sum(jnp.where(goes[k][:, None, None], held, 0), axis=0, dtype=BF16)
        pieces.append(shift(piece, "grp", k) if k > 0 else piece)
    right = jnp.sum(
        jnp.where(comes[:, None, None], jnp.stack(pieces), 0), axis=0, dtype=BF16
    )
    pieces, unused = gather_plane(right)
    whole = blank(place, (owned, width, rank))
    pieces, whole = lax.optimization_barrier((pieces, whole))

    blended = (momentum_decay * momentum.astype(F32) + gradient.astype(F32)).astype(BF16)
    keep = jnp.where(core == 0, blended[0], blended[1])
    give = jnp.where(core == 0, blended[1], blended[0])
    blocks = (keep, swap_core(give))

    projs, packed = project(place, *blocks, pieces)

    parts = packed.reshape(chips, packed.shape[0] // chips, BLOCK)
    part = jnp.sum(lax.all_to_all(parts, PLANE, 0, 0, tiled=True), axis=0)
    many = jnp.broadcast_to(part[None], (chips,) + part.shape)
    gram = lax.all_to_all(many, PLANE, 0, 0, tiled=True)
    inverse = inverse_factor(gram.reshape(-1, BLOCK), rank)

    bases, terms = partial(inverse, blocks, projs)
    terms = lax.all_to_all(terms, PLANE, 0, 0, tiled=True)
    rounded = jnp.sum(terms.astype(F32), axis=0).astype(BF16)

    theirs = (house == group)[None, :] & (owner_of[None, :] == after[:, None])
    theirs = jnp.any(theirs & (index % homed == 0)[None, :], axis=1)
    taken = (house[None, :] == before[:, None]) & (owner_of == group)[None, :]
    meta = jnp.stack(
        [
            jnp.any(taken, axis=1).astype(jnp.int32),
            jnp.sum(jnp.where(taken, slot[None, :], 0), axis=1, dtype=jnp.int32),
            jnp.sum(jnp.where(taken, index[None, :] % homed, 0), axis=1, dtype=jnp.int32),
            jnp.broadcast_to(core, (groups,)).astype(jnp.int32),
        ],
        axis=1,
    )
    half = share // 2
    lower, upper = rounded[:half], rounded[half:]
    stay = jnp.where(core == 0, lower, upper)
    other = swap_core(jnp.where(core == 0, upper, lower))
    both = jnp.concatenate(
        [jnp.where(core == 0, stay, other), jnp.where(core == 0, other, stay)], axis=0
    )
    piece = jnp.where(theirs[2:3, None], both[:half], both[half:])
    pieces, piece = gather_plane(both, shift(piece, "grp", 2))
    many = jnp.broadcast_to(piece[None], (chips, half, rank))
    many = lax.all_to_all(many, PLANE, 0, 0, tiled=True)
    both, *sends = split(place, theirs.astype(jnp.int32), pieces, homed)
    came = [shift(send, "grp", k) for send, k in zip(sends, (1, 3))]
    facing = swap_core(both)
    full, fresh = scale(place, both, facing)
    whole = put_expert(0, whole, meta, both, facing)
    full, whole = lax.optimization_barrier((full, whole))
    factor = math.sqrt(2 * rows_local * chips * width / rank)
    kept, moved = finish(factor, place, full, fresh, blocks, bases)
    whole = put_expert(2, whole, meta, many, swap_core(many))
    for k, value in zip((1, 3), came):
        whole = put_expert(k, whole, meta, value, swap_core(value))
    new_qfactor = whole

    outs = [put_rows(own, place, swap_core(give)) for own, give in zip(kept, moved)]
    return (*outs, new_qfactor)


def solution(mesh):
    fine = Mesh(mesh.devices.reshape(4, 4, 4, 2), ("grp", "y", "x", "core"))
    rows = P("grp", ROWS, None)
    return jax.shard_map(
        local,
        mesh=fine,
        in_specs=(rows, rows, P("grp", None, None), P()),
        out_specs=(rows, rows, P("grp", None, None)),
        check_vma=False,
    )
```

```python
import math

import jax
import jax.numpy as jnp
from jax import lax
from jax.experimental import pallas as pl
from jax.experimental.pallas import tpu as pltpu
from jax.sharding import Mesh
from jax.sharding import PartitionSpec as P

momentum_decay = 0.95
root_eps = 1e-06
HIGHEST = lax.Precision.HIGHEST
F32 = jnp.float32
BF16 = jnp.bfloat16
PLANE = ("y", "x")
ROWS = ("y", "x", "core")
BLOCK = 128


def eliminate(block):
    size = block.shape[0]
    lane = lax.broadcasted_iota(jnp.int32, (8, size), 1)
    sub = lax.broadcasted_iota(jnp.int32, (8, size), 0)
    count = size // 8

    def spread(tile, at):
        return jnp.broadcast_to(tile[:, at : at + 1], (8, size))

    def repeat(tile, at):
        return jnp.broadcast_to(tile[at : at + 1, :], (8, size))

    tiles = [block[8 * t : 8 * t + 8, :] for t in range(count)]
    done = []
    for t in range(count):
        base = 8 * t
        own = (lane >= base) & (lane < base + 8)
        columns = [spread(tiles[t], base + j) for j in range(8)]
        rows = jnp.where(own, jnp.where(lane == sub + base, 1.0, 0.0), tiles[t])
        result = None
        for k in range(8):
            here = sub == k
            inverse = 1.0 / repeat(columns[k], k)
            row = repeat(rows, k)
            value = row * jnp.sqrt(inverse)
            result = value if result is None else jnp.where(here, value, result)
            scaled = columns[k] * inverse
            for j in range(k + 1, 8):
                pivot = repeat(columns[j], k)
                columns[j] = jnp.where(here, pivot * inverse, columns[j] - scaled * pivot)
            rows = jnp.where(here, row * inverse, rows - scaled * row)
        done.append(jnp.where(lane <= sub + base, result, 0.0))
        solved = [repeat(rows, k) for k in range(8)]
        for u in range(t + 1, count):
            p = [spread(tiles[u], base + j) * solved[j] for j in range(8)]
            taken = ((p[0] + p[1]) + (p[2] + p[3])) + ((p[4] + p[5]) + (p[6] + p[7]))
            tiles[u] = jnp.where(own, 0.0, tiles[u]) - taken
    return jnp.concatenate(done, axis=0)


def dot(a, b, turned=False):
    return lax.dot_general(
        a,
        b,
        (((1,), (1 if turned else 0,)), ((), ())),
        precision=HIGHEST,
        preferred_element_type=F32,
    )


def product(a, b):
    return lax.dot_general(a, b, (((0,), (0,)), ((), ())), preferred_element_type=F32)


def call(kernel, name, out_shape, scratch=(), smem=0, flops=0, moved=0):
    def run(*args):
        specs = [
            pl.BlockSpec(memory_space=pltpu.SMEM if i < smem else pltpu.VMEM)
            for i in range(len(args))
        ]
        return pl.pallas_call(
            kernel,
            in_specs=specs,
            out_shape=out_shape,
            scratch_shapes=list(scratch),
            compiler_params=pltpu.CompilerParams(vmem_limit_bytes=24 * 1024 * 1024),
            cost_estimate=pl.CostEstimate(
                flops=flops, bytes_accessed=moved, transcendentals=0
            ),
            name=name,
        )(*args)

    return run


def shape(dims, dtype=F32):
    return jax.ShapeDtypeStruct(dims, dtype)


def assemble(place_ref, pieces, whole_ref):
    side = len(pieces) // 2
    share = pieces[0].shape[1]
    half = whole_ref.shape[1] // 2
    y, x = place_ref[0], place_ref[1]
    for i in range(side):
        for j in range(side):
            for part, (dy, dx) in enumerate(((i, j), (j, i))):
                chip = lax.rem(y + side - dy, side) * side + lax.rem(x + side - dx, side)
                at = pl.ds(pl.multiple_of(chip * share, share), share)
                piece = pieces[part * side + i]
                whole_ref[at, part * half : (part + 1) * half] = piece[j]


def project_kernel(place_ref, first_ref, second_ref, *refs):
    pieces, outs = refs[:8], refs[8:]
    proj_refs, packed_ref, right_ref = outs[:2], outs[2], outs[3]
    assemble(place_ref, pieces, right_ref)
    right = right_ref[...]
    rank = right.shape[1]
    projs = []
    for block_ref, proj_ref in zip((first_ref, second_ref), proj_refs):
        proj = jnp.dot(block_ref[...], right, preferred_element_type=F32)
        proj_ref[...] = proj
        projs.append(proj)
    place = 0
    for i in range(rank // BLOCK):
        lo, hi = i * BLOCK, (i + 1) * BLOCK
        wide = sum(
            lax.dot_general(
                proj[:, lo:hi],
                proj[:, :hi],
                (((0,), (0,)), ((), ())),
                precision=HIGHEST,
                preferred_element_type=F32,
            )
            for proj in projs
        )
        for j in range(i + 1):
            packed_ref[place * BLOCK : (place + 1) * BLOCK, :] = wide[
                :, j * BLOCK : (j + 1) * BLOCK
            ]
            place += 1


def project(place, first, second, pieces):
    rows, width = first.shape
    rank = 2 * pieces[0].shape[2]
    steps = rank // BLOCK
    packed = steps * (steps + 1) // 2 * BLOCK
    out = call(
        project_kernel,
        "project",
        [shape((rows, rank))] * 2 + [shape((packed, BLOCK))],
        [pltpu.VMEM((width, rank), BF16)],
        smem=1,
        flops=4_000_000_000,
        moved=6 * 1024 * 1024,
    )(place, first, second, *pieces)
    return out[:2], out[2]


def partial_kernel(inverse_ref, *refs):
    blocks, projs, bases, out_ref = refs[:2], refs[2:4], refs[4:6], refs[6]
    pieces, share, rank = out_ref.shape
    tile = 4
    inverse = inverse_ref[...]
    values = []
    for proj_ref, basis_ref in zip(projs, bases):
        basis = dot(proj_ref[...], inverse, turned=True).astype(BF16)
        basis_ref[...] = basis
        values.append(basis)

    def step(i, carry):
        at = pl.ds(pl.multiple_of(i * tile * share, tile * share), tile * share)
        total = sum(product(ref[:, at], basis) for ref, basis in zip(blocks, values))
        out_ref[pl.ds(i * tile, tile)] = total.astype(BF16).reshape(tile, share, rank)
        return carry

    lax.fori_loop(0, pieces // tile, step, 0)


def partial(inverse, blocks, projs):
    rows, rank = projs[0].shape
    width = blocks[0].shape[1]
    out = call(
        partial_kernel,
        "partial",
        [shape((rows, rank), BF16)] * 2 + [shape((16, width // 16, rank), BF16)],
        flops=3_000_000_000,
        moved=7 * 1024 * 1024,
    )(inverse, *blocks, *projs)
    return out[:2], out[2]


def factor_kernel(packed_ref, out_ref, work_ref):
    size = work_ref.shape[0]
    steps = size // BLOCK
    place = 0
    for i in range(steps):
        for j in range(i + 1):
            piece = packed_ref[place * BLOCK : (place + 1) * BLOCK, :]
            work_ref[i * BLOCK : (i + 1) * BLOCK, j * BLOCK : (j + 1) * BLOCK] = piece
            place += 1
    for j in range(steps):
        lo, hi = j * BLOCK, (j + 1) * BLOCK
        inverse = eliminate(work_ref[lo:hi, lo:hi])
        out_ref[lo:hi, lo:hi] = inverse
        if j > 0:
            out_ref[lo:hi, :lo] = dot(inverse, work_ref[lo:hi, :lo])
        if j < steps - 1:
            out_ref[lo:hi, hi:] = jnp.zeros((BLOCK, size - hi), F32)
            low = dot(work_ref[hi:, lo:hi], inverse, turned=True)
            if j > 0:
                work_ref[hi:, :lo] -= dot(low, out_ref[lo:hi, :lo])
            work_ref[hi:, lo:hi] = -dot(low, inverse)
            work_ref[hi:, hi:] -= dot(low, low, turned=True)


def inverse_factor(packed, rank):
    return call(
        factor_kernel,
        "inverse_factor",
        shape((rank, rank)),
        [pltpu.VMEM((rank, rank), F32)],
        flops=24_000_000_000,
        moved=2 * 1024 * 1024,
    )(packed)


def scale_halves(low_ref, high_ref, fresh_ref, full_ref=None, sent=None):
    chips, rows, rank = low_ref.shape
    step = 32
    width = 2 * chips * rows

    def add(chip, total):
        for ref in (low_ref, high_ref):
            for at in range(0, rows, step):
                value = ref[chip, at : at + step, :].astype(F32)
                total = total + jnp.sum(value * value, axis=0, keepdims=True)
        return total

    total = lax.fori_loop(0, chips, add, jnp.zeros((1, rank), F32), unroll=2)
    scaling = lax.rsqrt(total / width + root_eps)

    def store(chip, carry):
        for half, ref in enumerate((low_ref, high_ref)):
            for at in range(0, rows, step):
                value = ref[chip, at : at + step, :]
                start = pl.multiple_of((2 * chip + half) * rows + at, step)
                fresh_ref[pl.ds(start, step), :] = (value.astype(F32) * scaling).astype(BF16)
                if full_ref is not None:
                    full_ref[pl.ds(start, step), :] = value
        return carry

    parts = 4
    for part in range(parts):
        first, last = part * chips // parts, (part + 1) * chips // parts
        lax.fori_loop(first, last, store, 0, unroll=2)
        if sent is not None:
            sent(part, width // parts)


def split_kernel(place_ref, picks_ref, *refs):
    pieces, both_ref, sends, whole_ref = refs[:8], refs[8], refs[9:11], refs[11]
    assemble(place_ref, pieces, whole_ref)
    homed, chips, rows, rank = both_ref.shape
    for chip in range(chips):
        for h in range(homed):
            at = (chip * homed + h) * rows
            both_ref[h, chip] = whole_ref[at : at + rows, :]
    for send_ref, k in zip(sends, (1, 3)):
        send_ref[...] = both_ref[1 - picks_ref[k]]


def split(place, picks, pieces, homed):
    share, half = pieces[0].shape[1:]
    dims = (16, share // homed, 2 * half)
    return call(
        split_kernel,
        "split",
        [shape((homed,) + dims, BF16)] + [shape(dims, BF16)] * 2,
        [pltpu.VMEM((16 * share, 2 * half), BF16)],
        smem=2,
        flops=1_000_000,
        moved=6 * 1024 * 1024,
    )(place, picks, *pieces)


def scale_kernel(place_ref, both_ref, facing_ref, full_ref, fresh_ref):
    for first in range(2):

        @pl.when(place_ref[2] == first)
        def _():
            refs = (both_ref.at[first], facing_ref.at[first])
            scale_halves(refs[first], refs[1 - first], fresh_ref, full_ref)


def scale(place, both, facing):
    homed, chips, rows, rank = both.shape
    return call(
        scale_kernel,
        "scale",
        [shape((2 * chips * rows, rank), BF16)] * 2,
        smem=1,
        flops=10_000_000,
        moved=8 * 1024 * 1024,
    )(place, both, facing)


def finish_kernel(factor, place_ref, full_ref, fresh_ref, *refs):
    blocks, bases, wholes, gives = refs[:2], refs[2:4], refs[4:6], refs[6:8]
    stays, sems = refs[8:10], refs[10]
    full, fresh = full_ref[...], fresh_ref[...]
    along = (((1,), (1,)), ((), ()))
    copies = []
    for i in (1, 0):
        outs = gives if i == 1 else stays
        basis = bases[i][...]
        rounded = lax.dot_general(basis, full, along, preferred_element_type=F32)
        outs[0][...] = (
            blocks[i][...].astype(F32) - (1.0 - momentum_decay) * rounded
        ).astype(BF16)
        turned = lax.dot_general(basis, fresh, along, preferred_element_type=F32)
        outs[1][...] = (factor * turned).astype(BF16)
    for i in range(2):
        copy = pltpu.make_async_copy(stays[i], wholes[i].at[place_ref[2]], sems.at[i])
        copy.start()
        copies.append(copy)
    for copy in copies:
        copy.wait()


def finish(factor, place, full, fresh, blocks, bases):
    rows, width = blocks[0].shape
    vmem = pl.BlockSpec(memory_space=pltpu.VMEM)
    anywhere = pl.BlockSpec(memory_space=pl.ANY)
    out = pl.pallas_call(
        lambda *refs: finish_kernel(factor, *refs),
        in_specs=[pl.BlockSpec(memory_space=pltpu.SMEM)] + [vmem] * 6,
        out_specs=[anywhere] * 2 + [vmem] * 2,
        out_shape=[shape((2, rows, width), BF16)] * 2 + [shape((rows, width), BF16)] * 2,
        scratch_shapes=[pltpu.VMEM((rows, width), BF16)] * 2
        + [pltpu.SemaphoreType.DMA((2,))],
        compiler_params=pltpu.CompilerParams(vmem_limit_bytes=24 * 1024 * 1024),
        cost_estimate=pl.CostEstimate(
            flops=6_000_000_000, bytes_accessed=10 * 1024 * 1024, transcendentals=0
        ),
        name="finish",
    )(place, full, fresh, *blocks, *bases)
    return out[:2], out[2:]


def put_rows(whole, place, back):
    def kernel(place_ref, unused, back_ref, out_ref, sems):
        copy = pltpu.make_async_copy(back_ref, out_ref.at[1 - place_ref[2]], sems.at[0])
        copy.start()
        copy.wait()

    return put(kernel, "put_rows", whole, place, (back,))


def put(kernel, name, whole, meta, values, scratch=()):
    anywhere = pl.BlockSpec(memory_space=pl.ANY)
    smem = pl.BlockSpec(memory_space=pltpu.SMEM)
    return pl.pallas_call(
        kernel,
        in_specs=[smem, anywhere]
        + [pl.BlockSpec(memory_space=pltpu.VMEM)] * len(values),
        out_specs=anywhere,
        out_shape=shape(whole.shape, whole.dtype),
        input_output_aliases={1: 0},
        scratch_shapes=list(scratch) + [pltpu.SemaphoreType.DMA((4,))],
        compiler_params=pltpu.CompilerParams(vmem_limit_bytes=16 * 1024 * 1024),
        cost_estimate=pl.CostEstimate(
            flops=0, bytes_accessed=4 * 1024 * 1024, transcendentals=0
        ),
        name=name,
    )(meta, whole, *values)


def put_expert(k, whole, meta, mine, other):
    chips, rows, rank = mine.shape[-3:]

    def kernel(meta_ref, unused, mine_ref, other_ref, out_ref, new_ref, sems):
        parity = meta_ref[k, 2]

        def copy(part, size):
            at = pl.ds(part * size, size)
            return pltpu.make_async_copy(
                new_ref.at[at, :], out_ref.at[meta_ref[k, 1], at, :], sems.at[part]
            )

        for first in range(2):

            @pl.when((meta_ref[k, 0] == 1) & (meta_ref[k, 3] == first))
            def _():
                refs = (mine_ref, other_ref)
                if len(mine.shape) == 4:
                    refs = (mine_ref.at[parity], other_ref.at[parity])
                scale_halves(
                    refs[first],
                    refs[1 - first],
                    new_ref,
                    sent=lambda part, size: copy(part, size).start(),
                )
                for part in range(4):
                    copy(part, 2 * chips * rows // 4).wait()

    scratch = (pltpu.VMEM((2 * chips * rows, rank), BF16),)
    return put(kernel, "put_expert", whole, meta, (mine, other), scratch)


def blank(place, dims):
    def kernel(unused, out_ref, zero_ref, sems):
        zero_ref[...] = jnp.zeros_like(zero_ref)
        copies = [
            pltpu.make_async_copy(zero_ref, out_ref.at[i], sems.at[i])
            for i in range(dims[0])
        ]
        for copy in copies:
            copy.start()
        for copy in copies:
            copy.wait()

    return pl.pallas_call(
        kernel,
        in_specs=[pl.BlockSpec(memory_space=pltpu.SMEM)],
        out_specs=pl.BlockSpec(memory_space=pl.ANY),
        out_shape=shape(dims, BF16),
        scratch_shapes=[pltpu.VMEM(dims[1:], BF16), pltpu.SemaphoreType.DMA((dims[0],))],
        compiler_params=pltpu.CompilerParams(vmem_limit_bytes=16 * 1024 * 1024),
        cost_estimate=pl.CostEstimate(
            flops=0, bytes_accessed=8 * 1024 * 1024, transcendentals=0
        ),
        name="blank",
    )(place)


def swap_core(x):
    return lax.ppermute(x, "core", [(0, 1), (1, 0)])


def shift(x, axis, k):
    n = lax.axis_size(axis)
    return lax.ppermute(x, axis, [(i, (i + k) % n) for i in range(n)])


def around(x, axis):
    far = {k: shift(x, axis, k) for k in (2, 1, 3)}
    return [x] + [far[k] for k in (1, 2, 3)]


def gather_plane(x, beside=()):
    half = x.shape[1] // 2
    first = jnp.stack(around(x[:, :half], "x"))
    second = jnp.stack(around(x[:, half:], "y"))
    first, second, beside = lax.optimization_barrier((first, second, beside))
    return around(first, "y") + around(second, "x"), beside


def local(momentum, gradient, qfactor, owner_of):
    groups = lax.axis_size("grp")
    chips = lax.axis_size(PLANE)
    homed, rows_local, width = momentum.shape
    owned, unused, rank = qfactor.shape
    total = owner_of.shape[0]
    group = lax.axis_index("grp")
    core = lax.axis_index("core")
    chip = lax.axis_index(PLANE)
    place = jnp.stack([lax.axis_index("y"), lax.axis_index("x"), core]).astype(jnp.int32)

    index = jnp.arange(total, dtype=jnp.int32)
    same = owner_of[:, None] == owner_of[None, :]
    earlier = index[None, :] < index[:, None]
    slot = jnp.sum((same & earlier).astype(jnp.int32), axis=1)
    hops = jnp.arange(groups, dtype=jnp.int32)
    after = (group + hops) % groups
    before = (group - hops + groups) % groups
    slots = jnp.arange(owned, dtype=jnp.int32)
    house = index // homed
    in_slot = (slot[:, None] == slots[None, :]) & (owner_of == group)[:, None]
    this_core = index % homed == core

    share = width // chips
    held = lax.dynamic_slice(qfactor, (0, chip * share, 0), (owned, share, rank))
    goes = (house[None, :] == after[:, None]) & this_core[None, :]
    goes = jnp.any(goes[:, :, None] & in_slot[None, :, :], axis=1)
    comes = (house == group) & this_core
    comes = jnp.any(comes[None, :] & (owner_of[None, :] == before[:, None]), axis=1)
    pieces = []
    for k in range(groups):
        piece = jnp.sum(jnp.where(goes[k][:, None, None], held, 0), axis=0, dtype=BF16)
        pieces.append(shift(piece, "grp", k) if k > 0 else piece)
    right = jnp.sum(
        jnp.where(comes[:, None, None], jnp.stack(pieces), 0), axis=0, dtype=BF16
    )
    pieces, unused = gather_plane(right)
    whole = blank(place, (owned, width, rank))
    pieces, whole = lax.optimization_barrier((pieces, whole))

    blended = (momentum_decay * momentum.astype(F32) + gradient.astype(F32)).astype(BF16)
    keep = jnp.where(core == 0, blended[0], blended[1])
    give = jnp.where(core == 0, blended[1], blended[0])
    blocks = (keep, swap_core(give))

    projs, packed = project(place, *blocks, pieces)

    parts = packed.reshape(chips, packed.shape[0] // chips, BLOCK)
    part = jnp.sum(lax.all_to_all(parts, PLANE, 0, 0, tiled=True), axis=0)
    many = jnp.broadcast_to(part[None], (chips,) + part.shape)
    gram = lax.all_to_all(many, PLANE, 0, 0, tiled=True)
    inverse = inverse_factor(gram.reshape(-1, BLOCK), rank)

    bases, terms = partial(inverse, blocks, projs)
    terms = lax.all_to_all(terms, PLANE, 0, 0, tiled=True)
    rounded = jnp.sum(terms.astype(F32), axis=0).astype(BF16)

    half = share // 2
    lower, upper = rounded[:half], rounded[half:]
    stay = jnp.where(core == 0, lower, upper)
    other = swap_core(jnp.where(core == 0, upper, lower))
    both = jnp.concatenate(
        [jnp.where(core == 0, stay, other), jnp.where(core == 0, other, stay)], axis=0
    )

    theirs = (house == group)[None, :] & (owner_of[None, :] == after[:, None])
    theirs = jnp.any(theirs & (index % homed == 0)[None, :], axis=1)
    taken = (house[None, :] == before[:, None]) & (owner_of == group)[None, :]
    meta = jnp.stack(
        [
            jnp.any(taken, axis=1).astype(jnp.int32),
            jnp.sum(jnp.where(taken, slot[None, :], 0), axis=1, dtype=jnp.int32),
            jnp.sum(jnp.where(taken, index[None, :] % homed, 0), axis=1, dtype=jnp.int32),
            jnp.broadcast_to(core, (groups,)).astype(jnp.int32),
        ],
        axis=1,
    )
    piece = jnp.where(theirs[2:3, None], both[:half], both[half:])
    pieces, piece = gather_plane(both, shift(piece, "grp", 2))
    many = jnp.broadcast_to(piece[None], (chips, half, rank))
    many = lax.all_to_all(many, PLANE, 0, 0, tiled=True)
    both, *sends = split(place, theirs.astype(jnp.int32), pieces, homed)
    came = [shift(send, "grp", k) for send, k in zip(sends, (1, 3))]
    facing = swap_core(both)
    full, fresh = scale(place, both, facing)
    whole = put_expert(0, whole, meta, both, facing)
    full, whole = lax.optimization_barrier((full, whole))
    factor = math.sqrt(2 * rows_local * chips * width / rank)
    kept, moved = finish(factor, place, full, fresh, blocks, bases)
    many, came, kept, moved = lax.optimization_barrier((many, came, kept, moved))
    outs = [put_rows(own, place, swap_core(give)) for own, give in zip(kept, moved)]
    whole = put_expert(2, whole, meta, many, swap_core(many))
    for k, value in zip((1, 3), came):
        whole = put_expert(k, whole, meta, value, swap_core(value))
    new_qfactor = whole

    return (*outs, new_qfactor)


def solution(mesh):
    fine = Mesh(mesh.devices.reshape(4, 4, 4, 2), ("grp", "y", "x", "core"))
    rows = P("grp", ROWS, None)
    return jax.shard_map(
        local,
        mesh=fine,
        in_specs=(rows, rows, P("grp", None, None), P()),
        out_specs=(rows, rows, P("grp", None, None)),
        check_vma=False,
    )
```

```python
import math

import jax
import jax.numpy as jnp
from jax import lax
from jax.experimental import pallas as pl
from jax.experimental.pallas import tpu as pltpu
from jax.sharding import Mesh
from jax.sharding import PartitionSpec as P

momentum_decay = 0.95
root_eps = 1e-06
HIGHEST = lax.Precision.HIGHEST
F32 = jnp.float32
BF16 = jnp.bfloat16
PLANE = ("y", "x")
ROWS = ("y", "x", "core")
BLOCK = 128


def eliminate(block):
    size = block.shape[0]
    lane = lax.broadcasted_iota(jnp.int32, (8, size), 1)
    sub = lax.broadcasted_iota(jnp.int32, (8, size), 0)
    count = size // 8

    def spread(tile, at):
        return jnp.broadcast_to(tile[:, at : at + 1], (8, size))

    def repeat(tile, at):
        return jnp.broadcast_to(tile[at : at + 1, :], (8, size))

    tiles = [block[8 * t : 8 * t + 8, :] for t in range(count)]
    done = []
    for t in range(count):
        base = 8 * t
        own = (lane >= base) & (lane < base + 8)
        columns = [spread(tiles[t], base + j) for j in range(8)]
        rows = jnp.where(own, jnp.where(lane == sub + base, 1.0, 0.0), tiles[t])
        result = None
        for k in range(8):
            here = sub == k
            inverse = 1.0 / repeat(columns[k], k)
            row = repeat(rows, k)
            value = row * jnp.sqrt(inverse)
            result = value if result is None else jnp.where(here, value, result)
            scaled = columns[k] * inverse
            for j in range(k + 1, 8):
                pivot = repeat(columns[j], k)
                columns[j] = jnp.where(here, pivot * inverse, columns[j] - scaled * pivot)
            rows = jnp.where(here, row * inverse, rows - scaled * row)
        done.append(jnp.where(lane <= sub + base, result, 0.0))
        solved = [repeat(rows, k) for k in range(8)]
        for u in range(t + 1, count):
            p = [spread(tiles[u], base + j) * solved[j] for j in range(8)]
            taken = ((p[0] + p[1]) + (p[2] + p[3])) + ((p[4] + p[5]) + (p[6] + p[7]))
            tiles[u] = jnp.where(own, 0.0, tiles[u]) - taken
    return jnp.concatenate(done, axis=0)


def dot(a, b, turned=False):
    return lax.dot_general(
        a,
        b,
        (((1,), (1 if turned else 0,)), ((), ())),
        precision=HIGHEST,
        preferred_element_type=F32,
    )


def product(a, b):
    return lax.dot_general(a, b, (((0,), (0,)), ((), ())), preferred_element_type=F32)


def call(kernel, name, out_shape, scratch=(), smem=0, flops=0, moved=0):
    def run(*args):
        specs = [
            pl.BlockSpec(memory_space=pltpu.SMEM if i < smem else pltpu.VMEM)
            for i in range(len(args))
        ]
        return pl.pallas_call(
            kernel,
            in_specs=specs,
            out_shape=out_shape,
            scratch_shapes=list(scratch),
            compiler_params=pltpu.CompilerParams(vmem_limit_bytes=24 * 1024 * 1024),
            cost_estimate=pl.CostEstimate(
                flops=flops, bytes_accessed=moved, transcendentals=0
            ),
            name=name,
        )(*args)

    return run


def shape(dims, dtype=F32):
    return jax.ShapeDtypeStruct(dims, dtype)


def assemble(place_ref, pieces, whole_ref):
    side = len(pieces) // 2
    share = pieces[0].shape[1]
    half = whole_ref.shape[1] // 2
    y, x = place_ref[0], place_ref[1]
    for i in range(side):
        for j in range(side):
            for part, (dy, dx) in enumerate(((i, j), (j, i))):
                chip = lax.rem(y + side - dy, side) * side + lax.rem(x + side - dx, side)
                at = pl.ds(pl.multiple_of(chip * share, share), share)
                piece = pieces[part * side + i]
                whole_ref[at, part * half : (part + 1) * half] = piece[j]


def project_kernel(place_ref, first_ref, second_ref, *refs):
    pieces, outs = refs[:8], refs[8:]
    proj_refs, packed_ref, right_ref = outs[:2], outs[2], outs[3]
    assemble(place_ref, pieces, right_ref)
    right = right_ref[...]
    rank = right.shape[1]
    projs = []
    for block_ref, proj_ref in zip((first_ref, second_ref), proj_refs):
        proj = jnp.dot(block_ref[...], right, preferred_element_type=F32)
        proj_ref[...] = proj
        projs.append(proj)
    place = 0
    for i in range(rank // BLOCK):
        lo, hi = i * BLOCK, (i + 1) * BLOCK
        wide = sum(
            lax.dot_general(
                proj[:, lo:hi],
                proj[:, :hi],
                (((0,), (0,)), ((), ())),
                precision=HIGHEST,
                preferred_element_type=F32,
            )
            for proj in projs
        )
        for j in range(i + 1):
            packed_ref[place * BLOCK : (place + 1) * BLOCK, :] = wide[
                :, j * BLOCK : (j + 1) * BLOCK
            ]
            place += 1


def project(place, first, second, pieces):
    rows, width = first.shape
    rank = 2 * pieces[0].shape[2]
    steps = rank // BLOCK
    packed = steps * (steps + 1) // 2 * BLOCK
    out = call(
        project_kernel,
        "project",
        [shape((rows, rank))] * 2 + [shape((packed, BLOCK))],
        [pltpu.VMEM((width, rank), BF16)],
        smem=1,
        flops=4_000_000_000,
        moved=6 * 1024 * 1024,
    )(place, first, second, *pieces)
    return out[:2], out[2]


def partial_kernel(inverse_ref, *refs):
    blocks, projs, bases, out_ref = refs[:2], refs[2:4], refs[4:6], refs[6]
    pieces, share, rank = out_ref.shape
    tile = 4
    inverse = inverse_ref[...]
    values = []
    for proj_ref, basis_ref in zip(projs, bases):
        basis = dot(proj_ref[...], inverse, turned=True).astype(BF16)
        basis_ref[...] = basis
        values.append(basis)

    def step(i, carry):
        at = pl.ds(pl.multiple_of(i * tile * share, tile * share), tile * share)
        total = sum(product(ref[:, at], basis) for ref, basis in zip(blocks, values))
        out_ref[pl.ds(i * tile, tile)] = total.astype(BF16).reshape(tile, share, rank)
        return carry

    lax.fori_loop(0, pieces // tile, step, 0)


def partial(inverse, blocks, projs):
    rows, rank = projs[0].shape
    width = blocks[0].shape[1]
    out = call(
        partial_kernel,
        "partial",
        [shape((rows, rank), BF16)] * 2 + [shape((16, width // 16, rank), BF16)],
        flops=3_000_000_000,
        moved=7 * 1024 * 1024,
    )(inverse, *blocks, *projs)
    return out[:2], out[2]


def factor_kernel(packed_ref, out_ref, work_ref):
    size = work_ref.shape[0]
    steps = size // BLOCK
    place = 0
    for i in range(steps):
        for j in range(i + 1):
            piece = packed_ref[place * BLOCK : (place + 1) * BLOCK, :]
            work_ref[i * BLOCK : (i + 1) * BLOCK, j * BLOCK : (j + 1) * BLOCK] = piece
            place += 1
    for j in range(steps):
        lo, hi = j * BLOCK, (j + 1) * BLOCK
        inverse = eliminate(work_ref[lo:hi, lo:hi])
        out_ref[lo:hi, lo:hi] = inverse
        if j > 0:
            out_ref[lo:hi, :lo] = dot(inverse, work_ref[lo:hi, :lo])
        if j < steps - 1:
            out_ref[lo:hi, hi:] = jnp.zeros((BLOCK, size - hi), F32)
            low = dot(work_ref[hi:, lo:hi], inverse, turned=True)
            for i in range(j + 1, steps):
                start, end = (i - j - 1) * BLOCK, (i - j) * BLOCK
                at = slice(i * BLOCK, (i + 1) * BLOCK)
                taken = dot(low[start:end], low[:end], turned=True)
                work_ref[at, hi : (i + 1) * BLOCK] -= taken
            work_ref[hi:, lo:hi] = -dot(low, inverse)
            if j > 0:
                work_ref[hi:, :lo] -= dot(low, out_ref[lo:hi, :lo])


def inverse_factor(packed, rank):
    return call(
        factor_kernel,
        "inverse_factor",
        shape((rank, rank)),
        [pltpu.VMEM((rank, rank), F32)],
        flops=24_000_000_000,
        moved=2 * 1024 * 1024,
    )(packed)


def scale_halves(low_ref, high_ref, fresh_ref, full_ref=None, sent=None):
    chips, rows, rank = low_ref.shape
    step = 32
    width = 2 * chips * rows

    def add(chip, total):
        for ref in (low_ref, high_ref):
            for at in range(0, rows, step):
                value = ref[chip, at : at + step, :].astype(F32)
                total = total + jnp.sum(value * value, axis=0, keepdims=True)
        return total

    total = lax.fori_loop(0, chips, add, jnp.zeros((1, rank), F32), unroll=2)
    scaling = lax.rsqrt(total / width + root_eps)

    def store(chip, carry):
        for half, ref in enumerate((low_ref, high_ref)):
            for at in range(0, rows, step):
                value = ref[chip, at : at + step, :]
                start = pl.multiple_of((2 * chip + half) * rows + at, step)
                fresh_ref[pl.ds(start, step), :] = (value.astype(F32) * scaling).astype(BF16)
                if full_ref is not None:
                    full_ref[pl.ds(start, step), :] = value
        return carry

    parts = 4
    for part in range(parts):
        first, last = part * chips // parts, (part + 1) * chips // parts
        lax.fori_loop(first, last, store, 0, unroll=2)
        if sent is not None:
            sent(part, width // parts)


def split_kernel(place_ref, picks_ref, *refs):
    pieces, both_ref, sends, whole_ref = refs[:8], refs[8], refs[9:11], refs[11]
    assemble(place_ref, pieces, whole_ref)
    homed, chips, rows, rank = both_ref.shape
    for chip in range(chips):
        for h in range(homed):
            at = (chip * homed + h) * rows
            both_ref[h, chip] = whole_ref[at : at + rows, :]
    for send_ref, k in zip(sends, (1, 3)):
        send_ref[...] = both_ref[1 - picks_ref[k]]


def split(place, picks, pieces, homed):
    share, half = pieces[0].shape[1:]
    dims = (16, share // homed, 2 * half)
    return call(
        split_kernel,
        "split",
        [shape((homed,) + dims, BF16)] + [shape(dims, BF16)] * 2,
        [pltpu.VMEM((16 * share, 2 * half), BF16)],
        smem=2,
        flops=1_000_000,
        moved=6 * 1024 * 1024,
    )(place, picks, *pieces)


def scale_kernel(place_ref, both_ref, facing_ref, full_ref, fresh_ref):
    for first in range(2):

        @pl.when(place_ref[2] == first)
        def _():
            refs = (both_ref.at[first], facing_ref.at[first])
            scale_halves(refs[first], refs[1 - first], fresh_ref, full_ref)


def scale(place, both, facing):
    homed, chips, rows, rank = both.shape
    return call(
        scale_kernel,
        "scale",
        [shape((2 * chips * rows, rank), BF16)] * 2,
        smem=1,
        flops=10_000_000,
        moved=8 * 1024 * 1024,
    )(place, both, facing)


def finish_kernel(factor, place_ref, full_ref, fresh_ref, *refs):
    blocks, bases, wholes, gives = refs[:2], refs[2:4], refs[4:6], refs[6:8]
    stays, sems = refs[8:10], refs[10]
    full, fresh = full_ref[...], fresh_ref[...]
    along = (((1,), (1,)), ((), ()))
    copies = []
    for i in (1, 0):
        outs = gives if i == 1 else stays
        basis = bases[i][...]
        rounded = lax.dot_general(basis, full, along, preferred_element_type=F32)
        outs[0][...] = (
            blocks[i][...].astype(F32) - (1.0 - momentum_decay) * rounded
        ).astype(BF16)
        turned = lax.dot_general(basis, fresh, along, preferred_element_type=F32)
        outs[1][...] = (factor * turned).astype(BF16)
    for i in range(2):
        copy = pltpu.make_async_copy(stays[i], wholes[i].at[place_ref[2]], sems.at[i])
        copy.start()
        copies.append(copy)
    for copy in copies:
        copy.wait()


def finish(factor, place, full, fresh, blocks, bases):
    rows, width = blocks[0].shape
    vmem = pl.BlockSpec(memory_space=pltpu.VMEM)
    anywhere = pl.BlockSpec(memory_space=pl.ANY)
    out = pl.pallas_call(
        lambda *refs: finish_kernel(factor, *refs),
        in_specs=[pl.BlockSpec(memory_space=pltpu.SMEM)] + [vmem] * 6,
        out_specs=[anywhere] * 2 + [vmem] * 2,
        out_shape=[shape((2, rows, width), BF16)] * 2 + [shape((rows, width), BF16)] * 2,
        scratch_shapes=[pltpu.VMEM((rows, width), BF16)] * 2
        + [pltpu.SemaphoreType.DMA((2,))],
        compiler_params=pltpu.CompilerParams(vmem_limit_bytes=24 * 1024 * 1024),
        cost_estimate=pl.CostEstimate(
            flops=6_000_000_000, bytes_accessed=10 * 1024 * 1024, transcendentals=0
        ),
        name="finish",
    )(place, full, fresh, *blocks, *bases)
    return out[:2], out[2:]


def put_rows(whole, place, back):
    def kernel(place_ref, unused, back_ref, out_ref, sems):
        copy = pltpu.make_async_copy(back_ref, out_ref.at[1 - place_ref[2]], sems.at[0])
        copy.start()
        copy.wait()

    return put(kernel, "put_rows", whole, place, (back,))


def put(kernel, name, whole, meta, values, scratch=()):
    anywhere = pl.BlockSpec(memory_space=pl.ANY)
    smem = pl.BlockSpec(memory_space=pltpu.SMEM)
    return pl.pallas_call(
        kernel,
        in_specs=[smem, anywhere]
        + [pl.BlockSpec(memory_space=pltpu.VMEM)] * len(values),
        out_specs=anywhere,
        out_shape=shape(whole.shape, whole.dtype),
        input_output_aliases={1: 0},
        scratch_shapes=list(scratch) + [pltpu.SemaphoreType.DMA((4,))],
        compiler_params=pltpu.CompilerParams(vmem_limit_bytes=16 * 1024 * 1024),
        cost_estimate=pl.CostEstimate(
            flops=0, bytes_accessed=4 * 1024 * 1024, transcendentals=0
        ),
        name=name,
    )(meta, whole, *values)


def put_expert(k, whole, meta, mine, other):
    chips, rows, rank = mine.shape[-3:]

    def kernel(meta_ref, unused, mine_ref, other_ref, out_ref, new_ref, sems):
        parity = meta_ref[k, 2]

        def copy(part, size):
            at = pl.ds(part * size, size)
            return pltpu.make_async_copy(
                new_ref.at[at, :], out_ref.at[meta_ref[k, 1], at, :], sems.at[part]
            )

        for first in range(2):

            @pl.when((meta_ref[k, 0] == 1) & (meta_ref[k, 3] == first))
            def _():
                refs = (mine_ref, other_ref)
                if len(mine.shape) == 4:
                    refs = (mine_ref.at[parity], other_ref.at[parity])
                scale_halves(
                    refs[first],
                    refs[1 - first],
                    new_ref,
                    sent=lambda part, size: copy(part, size).start(),
                )
                for part in range(4):
                    copy(part, 2 * chips * rows // 4).wait()

    scratch = (pltpu.VMEM((2 * chips * rows, rank), BF16),)
    return put(kernel, "put_expert", whole, meta, (mine, other), scratch)


def blank(place, dims):
    def kernel(unused, out_ref, zero_ref, sems):
        zero_ref[...] = jnp.zeros_like(zero_ref)
        copies = [
            pltpu.make_async_copy(zero_ref, out_ref.at[i], sems.at[i])
            for i in range(dims[0])
        ]
        for copy in copies:
            copy.start()
        for copy in copies:
            copy.wait()

    return pl.pallas_call(
        kernel,
        in_specs=[pl.BlockSpec(memory_space=pltpu.SMEM)],
        out_specs=pl.BlockSpec(memory_space=pl.ANY),
        out_shape=shape(dims, BF16),
        scratch_shapes=[pltpu.VMEM(dims[1:], BF16), pltpu.SemaphoreType.DMA((dims[0],))],
        compiler_params=pltpu.CompilerParams(vmem_limit_bytes=16 * 1024 * 1024),
        cost_estimate=pl.CostEstimate(
            flops=0, bytes_accessed=8 * 1024 * 1024, transcendentals=0
        ),
        name="blank",
    )(place)


def swap_core(x):
    return lax.ppermute(x, "core", [(0, 1), (1, 0)])


def shift(x, axis, k):
    n = lax.axis_size(axis)
    return lax.ppermute(x, axis, [(i, (i + k) % n) for i in range(n)])


def around(x, axis):
    far = {k: shift(x, axis, k) for k in (2, 1, 3)}
    return [x] + [far[k] for k in (1, 2, 3)]


def gather_plane(x, beside=()):
    half = x.shape[1] // 2
    first = jnp.stack(around(x[:, :half], "x"))
    second = jnp.stack(around(x[:, half:], "y"))
    first, second, beside = lax.optimization_barrier((first, second, beside))
    return around(first, "y") + around(second, "x"), beside


def local(momentum, gradient, qfactor, owner_of):
    groups = lax.axis_size("grp")
    chips = lax.axis_size(PLANE)
    homed, rows_local, width = momentum.shape
    owned, unused, rank = qfactor.shape
    total = owner_of.shape[0]
    group = lax.axis_index("grp")
    core = lax.axis_index("core")
    chip = lax.axis_index(PLANE)
    place = jnp.stack([lax.axis_index("y"), lax.axis_index("x"), core]).astype(jnp.int32)

    index = jnp.arange(total, dtype=jnp.int32)
    same = owner_of[:, None] == owner_of[None, :]
    earlier = index[None, :] < index[:, None]
    slot = jnp.sum((same & earlier).astype(jnp.int32), axis=1)
    hops = jnp.arange(groups, dtype=jnp.int32)
    after = (group + hops) % groups
    before = (group - hops + groups) % groups
    slots = jnp.arange(owned, dtype=jnp.int32)
    house = index // homed
    in_slot = (slot[:, None] == slots[None, :]) & (owner_of == group)[:, None]
    this_core = index % homed == core

    share = width // chips
    held = lax.dynamic_slice(qfactor, (0, chip * share, 0), (owned, share, rank))
    goes = (house[None, :] == after[:, None]) & this_core[None, :]
    goes = jnp.any(goes[:, :, None] & in_slot[None, :, :], axis=1)
    comes = (house == group) & this_core
    comes = jnp.any(comes[None, :] & (owner_of[None, :] == before[:, None]), axis=1)
    pieces = []
    for k in range(groups):
        piece = jnp.sum(jnp.where(goes[k][:, None, None], held, 0), axis=0, dtype=BF16)
        pieces.append(shift(piece, "grp", k) if k > 0 else piece)
    right = jnp.sum(
        jnp.where(comes[:, None, None], jnp.stack(pieces), 0), axis=0, dtype=BF16
    )
    pieces, unused = gather_plane(right)
    whole = blank(place, (owned, width, rank))
    pieces, whole = lax.optimization_barrier((pieces, whole))

    blended = (momentum_decay * momentum.astype(F32) + gradient.astype(F32)).astype(BF16)
    keep = jnp.where(core == 0, blended[0], blended[1])
    give = jnp.where(core == 0, blended[1], blended[0])
    blocks = (keep, swap_core(give))

    projs, packed = project(place, *blocks, pieces)

    parts = packed.reshape(chips, packed.shape[0] // chips, BLOCK)
    part = jnp.sum(lax.all_to_all(parts, PLANE, 0, 0, tiled=True), axis=0)
    many = jnp.broadcast_to(part[None], (chips,) + part.shape)
    gram = lax.all_to_all(many, PLANE, 0, 0, tiled=True)
    inverse = inverse_factor(gram.reshape(-1, BLOCK), rank)

    bases, terms = partial(inverse, blocks, projs)
    terms = lax.all_to_all(terms, PLANE, 0, 0, tiled=True)
    rounded = jnp.sum(terms.astype(F32), axis=0).astype(BF16)

    half = share // 2
    lower, upper = rounded[:half], rounded[half:]
    stay = jnp.where(core == 0, lower, upper)
    other = swap_core(jnp.where(core == 0, upper, lower))
    both = jnp.concatenate(
        [jnp.where(core == 0, stay, other), jnp.where(core == 0, other, stay)], axis=0
    )

    theirs = (house == group)[None, :] & (owner_of[None, :] == after[:, None])
    theirs = jnp.any(theirs & (index % homed == 0)[None, :], axis=1)
    taken = (house[None, :] == before[:, None]) & (owner_of == group)[None, :]
    meta = jnp.stack(
        [
            jnp.any(taken, axis=1).astype(jnp.int32),
            jnp.sum(jnp.where(taken, slot[None, :], 0), axis=1, dtype=jnp.int32),
            jnp.sum(jnp.where(taken, index[None, :] % homed, 0), axis=1, dtype=jnp.int32),
            jnp.broadcast_to(core, (groups,)).astype(jnp.int32),
        ],
        axis=1,
    )
    piece = jnp.where(theirs[2:3, None], both[:half], both[half:])
    pieces, piece = gather_plane(both, shift(piece, "grp", 2))
    many = jnp.broadcast_to(piece[None], (chips, half, rank))
    many = lax.all_to_all(many, PLANE, 0, 0, tiled=True)
    both, *sends = split(place, theirs.astype(jnp.int32), pieces, homed)
    came = [shift(send, "grp", k) for send, k in zip(sends, (1, 3))]
    facing = swap_core(both)
    full, fresh = scale(place, both, facing)
    whole = put_expert(0, whole, meta, both, facing)
    full, whole = lax.optimization_barrier((full, whole))
    factor = math.sqrt(2 * rows_local * chips * width / rank)
    kept, moved = finish(factor, place, full, fresh, blocks, bases)
    many, came, kept, moved = lax.optimization_barrier((many, came, kept, moved))
    outs = [put_rows(own, place, swap_core(give)) for own, give in zip(kept, moved)]
    whole = put_expert(2, whole, meta, many, swap_core(many))
    for k, value in zip((1, 3), came):
        whole = put_expert(k, whole, meta, value, swap_core(value))
    new_qfactor = whole

    return (*outs, new_qfactor)


def solution(mesh):
    fine = Mesh(mesh.devices.reshape(4, 4, 4, 2), ("grp", "y", "x", "core"))
    rows = P("grp", ROWS, None)
    return jax.shard_map(
        local,
        mesh=fine,
        in_specs=(rows, rows, P("grp", None, None), P()),
        out_specs=(rows, rows, P("grp", None, None)),
        check_vma=False,
    )
```

```python
import math

import jax
import jax.numpy as jnp
from jax import lax
from jax.experimental import pallas as pl
from jax.experimental.pallas import tpu as pltpu
from jax.sharding import Mesh
from jax.sharding import PartitionSpec as P

momentum_decay = 0.95
root_eps = 1e-06
HIGHEST = lax.Precision.HIGHEST
F32 = jnp.float32
BF16 = jnp.bfloat16
PLANE = ("y", "x")
ROWS = ("y", "x", "core")
BLOCK = 128


def eliminate(block):
    size = block.shape[0]
    lane = lax.broadcasted_iota(jnp.int32, (8, size), 1)
    sub = lax.broadcasted_iota(jnp.int32, (8, size), 0)
    count = size // 8

    def spread(tile, at):
        return jnp.broadcast_to(tile[:, at : at + 1], (8, size))

    def repeat(tile, at):
        return jnp.broadcast_to(tile[at : at + 1, :], (8, size))

    tiles = [block[8 * t : 8 * t + 8, :] for t in range(count)]
    done = []
    for t in range(count):
        base = 8 * t
        own = (lane >= base) & (lane < base + 8)
        columns = [spread(tiles[t], base + j) for j in range(8)]
        rows = jnp.where(own, jnp.where(lane == sub + base, 1.0, 0.0), tiles[t])
        result = None
        for k in range(8):
            here = sub == k
            inverse = 1.0 / repeat(columns[k], k)
            row = repeat(rows, k)
            value = row * jnp.sqrt(inverse)
            result = value if result is None else jnp.where(here, value, result)
            scaled = columns[k] * inverse
            for j in range(k + 1, 8):
                pivot = repeat(columns[j], k)
                columns[j] = jnp.where(here, pivot * inverse, columns[j] - scaled * pivot)
            rows = jnp.where(here, row * inverse, rows - scaled * row)
        done.append(jnp.where(lane <= sub + base, result, 0.0))
        solved = [repeat(rows, k) for k in range(8)]
        for u in range(t + 1, count):
            p = [spread(tiles[u], base + j) * solved[j] for j in range(8)]
            taken = ((p[0] + p[1]) + (p[2] + p[3])) + ((p[4] + p[5]) + (p[6] + p[7]))
            tiles[u] = jnp.where(own, 0.0, tiles[u]) - taken
    return jnp.concatenate(done, axis=0)


def dot(a, b, turned=False):
    return lax.dot_general(
        a,
        b,
        (((1,), (1 if turned else 0,)), ((), ())),
        precision=HIGHEST,
        preferred_element_type=F32,
    )


def product(a, b):
    return lax.dot_general(a, b, (((0,), (0,)), ((), ())), preferred_element_type=F32)


def call(kernel, name, out_shape, scratch=(), smem=0, flops=0, moved=0):
    def run(*args):
        specs = [
            pl.BlockSpec(memory_space=pltpu.SMEM if i < smem else pltpu.VMEM)
            for i in range(len(args))
        ]
        return pl.pallas_call(
            kernel,
            in_specs=specs,
            out_shape=out_shape,
            scratch_shapes=list(scratch),
            compiler_params=pltpu.CompilerParams(vmem_limit_bytes=24 * 1024 * 1024),
            cost_estimate=pl.CostEstimate(
                flops=flops, bytes_accessed=moved, transcendentals=0
            ),
            name=name,
        )(*args)

    return run


def shape(dims, dtype=F32):
    return jax.ShapeDtypeStruct(dims, dtype)


def assemble(place_ref, pieces, whole_ref):
    side = len(pieces) // 2
    share = pieces[0].shape[1]
    half = whole_ref.shape[1] // 2
    y, x = place_ref[0], place_ref[1]
    for i in range(side):
        for j in range(side):
            for part, (dy, dx) in enumerate(((i, j), (j, i))):
                chip = lax.rem(y + side - dy, side) * side + lax.rem(x + side - dx, side)
                at = pl.ds(pl.multiple_of(chip * share, share), share)
                piece = pieces[part * side + i]
                whole_ref[at, part * half : (part + 1) * half] = piece[j]


def project_kernel(place_ref, first_ref, second_ref, *refs):
    pieces, outs = refs[:8], refs[8:]
    proj_refs, packed_ref, right_ref = outs[:2], outs[2], outs[3]
    assemble(place_ref, pieces, right_ref)
    right = right_ref[...]
    rank = right.shape[1]
    projs = []
    for block_ref, proj_ref in zip((first_ref, second_ref), proj_refs):
        proj = jnp.dot(block_ref[...], right, preferred_element_type=F32)
        proj_ref[...] = proj
        projs.append(proj)
    place = 0
    for i in range(rank // BLOCK):
        lo, hi = i * BLOCK, (i + 1) * BLOCK
        wide = sum(
            lax.dot_general(
                proj[:, lo:hi],
                proj[:, :hi],
                (((0,), (0,)), ((), ())),
                precision=HIGHEST,
                preferred_element_type=F32,
            )
            for proj in projs
        )
        for j in range(i + 1):
            packed_ref[place * BLOCK : (place + 1) * BLOCK, :] = wide[
                :, j * BLOCK : (j + 1) * BLOCK
            ]
            place += 1


def project(place, first, second, pieces):
    rows, width = first.shape
    rank = 2 * pieces[0].shape[2]
    steps = rank // BLOCK
    packed = steps * (steps + 1) // 2 * BLOCK
    out = call(
        project_kernel,
        "project",
        [shape((rows, rank))] * 2 + [shape((packed, BLOCK))],
        [pltpu.VMEM((width, rank), BF16)],
        smem=1,
        flops=4_000_000_000,
        moved=6 * 1024 * 1024,
    )(place, first, second, *pieces)
    return out[:2], out[2]


def partial_kernel(inverse_ref, *refs):
    blocks, projs, bases, out_ref = refs[:2], refs[2:4], refs[4:6], refs[6]
    pieces, share, rank = out_ref.shape
    tile = 4
    inverse = inverse_ref[...]
    values = []
    for proj_ref, basis_ref in zip(projs, bases):
        basis = dot(proj_ref[...], inverse, turned=True).astype(BF16)
        basis_ref[...] = basis
        values.append(basis)

    def step(i, carry):
        at = pl.ds(pl.multiple_of(i * tile * share, tile * share), tile * share)
        total = sum(product(ref[:, at], basis) for ref, basis in zip(blocks, values))
        out_ref[pl.ds(i * tile, tile)] = total.astype(BF16).reshape(tile, share, rank)
        return carry

    lax.fori_loop(0, pieces // tile, step, 0)


def partial(inverse, blocks, projs):
    rows, rank = projs[0].shape
    width = blocks[0].shape[1]
    out = call(
        partial_kernel,
        "partial",
        [shape((rows, rank), BF16)] * 2 + [shape((16, width // 16, rank), BF16)],
        flops=3_000_000_000,
        moved=7 * 1024 * 1024,
    )(inverse, *blocks, *projs)
    return out[:2], out[2]


def factor_kernel(packed_ref, out_ref, work_ref):
    size = work_ref.shape[0]
    steps = size // BLOCK
    place = 0
    for i in range(steps):
        for j in range(i + 1):
            piece = packed_ref[place * BLOCK : (place + 1) * BLOCK, :]
            work_ref[i * BLOCK : (i + 1) * BLOCK, j * BLOCK : (j + 1) * BLOCK] = piece
            place += 1
    for j in range(steps):
        lo, hi = j * BLOCK, (j + 1) * BLOCK
        inverse = eliminate(work_ref[lo:hi, lo:hi])
        out_ref[lo:hi, lo:hi] = inverse
        if j > 0:
            out_ref[lo:hi, :lo] = dot(inverse, work_ref[lo:hi, :lo])
        if j < steps - 1:
            out_ref[lo:hi, hi:] = jnp.zeros((BLOCK, size - hi), F32)
            low = dot(work_ref[hi:, lo:hi], inverse, turned=True)
            for i in range(j + 1, steps):
                start, end = (i - j - 1) * BLOCK, (i - j) * BLOCK
                at = slice(i * BLOCK, (i + 1) * BLOCK)
                taken = dot(low[start:end], low[:end], turned=True)
                work_ref[at, hi : (i + 1) * BLOCK] -= taken
            work_ref[hi:, lo:hi] = -dot(low, inverse)
            if j > 0:
                work_ref[hi:, :lo] -= dot(low, out_ref[lo:hi, :lo])


def inverse_factor(packed, rank):
    return call(
        factor_kernel,
        "inverse_factor",
        shape((rank, rank)),
        [pltpu.VMEM((rank, rank), F32)],
        flops=24_000_000_000,
        moved=2 * 1024 * 1024,
    )(packed)


def scale_halves(low_ref, high_ref, fresh_ref, full_ref=None, sent=None):
    chips, rows, rank = low_ref.shape
    step = 32
    width = 2 * chips * rows

    def add(chip, total):
        for ref in (low_ref, high_ref):
            for at in range(0, rows, step):
                value = ref[chip, at : at + step, :].astype(F32)
                total = total + jnp.sum(value * value, axis=0, keepdims=True)
        return total

    total = lax.fori_loop(0, chips, add, jnp.zeros((1, rank), F32), unroll=2)
    scaling = lax.rsqrt(total / width + root_eps)

    def store(chip, carry):
        for half, ref in enumerate((low_ref, high_ref)):
            for at in range(0, rows, step):
                value = ref[chip, at : at + step, :]
                start = pl.multiple_of((2 * chip + half) * rows + at, step)
                fresh_ref[pl.ds(start, step), :] = (value.astype(F32) * scaling).astype(BF16)
                if full_ref is not None:
                    full_ref[pl.ds(start, step), :] = value
        return carry

    parts = 4
    for part in range(parts):
        first, last = part * chips // parts, (part + 1) * chips // parts
        lax.fori_loop(first, last, store, 0, unroll=2)
        if sent is not None:
            sent(part, width // parts)


def split_kernel(place_ref, picks_ref, *refs):
    pieces, both_ref, sends, whole_ref = refs[:8], refs[8], refs[9:11], refs[11]
    assemble(place_ref, pieces, whole_ref)
    homed, chips, rows, rank = both_ref.shape
    for chip in range(chips):
        for h in range(homed):
            at = (chip * homed + h) * rows
            both_ref[h, chip] = whole_ref[at : at + rows, :]
    for send_ref, k in zip(sends, (1, 3)):
        send_ref[...] = both_ref[1 - picks_ref[k]]


def split(place, picks, pieces, homed):
    share, half = pieces[0].shape[1:]
    dims = (16, share // homed, 2 * half)
    return call(
        split_kernel,
        "split",
        [shape((homed,) + dims, BF16)] + [shape(dims, BF16)] * 2,
        [pltpu.VMEM((16 * share, 2 * half), BF16)],
        smem=2,
        flops=1_000_000,
        moved=6 * 1024 * 1024,
    )(place, picks, *pieces)


def scale_kernel(place_ref, both_ref, facing_ref, full_ref, fresh_ref):
    for first in range(2):

        @pl.when(place_ref[2] == first)
        def _():
            refs = (both_ref.at[first], facing_ref.at[first])
            scale_halves(refs[first], refs[1 - first], fresh_ref, full_ref)


def scale(place, both, facing):
    homed, chips, rows, rank = both.shape
    return call(
        scale_kernel,
        "scale",
        [shape((2 * chips * rows, rank), BF16)] * 2,
        smem=1,
        flops=10_000_000,
        moved=8 * 1024 * 1024,
    )(place, both, facing)


def finish_kernel(factor, place_ref, full_ref, fresh_ref, *refs):
    blocks, bases, wholes, gives = refs[:2], refs[2:4], refs[4:6], refs[6:8]
    stays, sems = refs[8:10], refs[10]
    full, fresh = full_ref[...], fresh_ref[...]
    along = (((1,), (1,)), ((), ()))
    copies = []
    for i in (1, 0):
        outs = gives if i == 1 else stays
        basis = bases[i][...]
        rounded = lax.dot_general(basis, full, along, preferred_element_type=F32)
        outs[0][...] = (
            blocks[i][...].astype(F32) - (1.0 - momentum_decay) * rounded
        ).astype(BF16)
        turned = lax.dot_general(basis, fresh, along, preferred_element_type=F32)
        outs[1][...] = (factor * turned).astype(BF16)
    for i in range(2):
        copy = pltpu.make_async_copy(stays[i], wholes[i].at[place_ref[2]], sems.at[i])
        copy.start()
        copies.append(copy)
    for copy in copies:
        copy.wait()


def finish(factor, place, full, fresh, blocks, bases):
    rows, width = blocks[0].shape
    vmem = pl.BlockSpec(memory_space=pltpu.VMEM)
    anywhere = pl.BlockSpec(memory_space=pl.ANY)
    out = pl.pallas_call(
        lambda *refs: finish_kernel(factor, *refs),
        in_specs=[pl.BlockSpec(memory_space=pltpu.SMEM)] + [vmem] * 6,
        out_specs=[anywhere] * 2 + [vmem] * 2,
        out_shape=[shape((2, rows, width), BF16)] * 2 + [shape((rows, width), BF16)] * 2,
        scratch_shapes=[pltpu.VMEM((rows, width), BF16)] * 2
        + [pltpu.SemaphoreType.DMA((2,))],
        compiler_params=pltpu.CompilerParams(vmem_limit_bytes=24 * 1024 * 1024),
        cost_estimate=pl.CostEstimate(
            flops=6_000_000_000, bytes_accessed=10 * 1024 * 1024, transcendentals=0
        ),
        name="finish",
    )(place, full, fresh, *blocks, *bases)
    return out[:2], out[2:]


def put_rows(whole, place, back):
    def kernel(place_ref, unused, back_ref, out_ref, sems):
        copy = pltpu.make_async_copy(back_ref, out_ref.at[1 - place_ref[2]], sems.at[0])
        copy.start()
        copy.wait()

    return put(kernel, "put_rows", whole, place, (back,))


def put(kernel, name, whole, meta, values, scratch=()):
    anywhere = pl.BlockSpec(memory_space=pl.ANY)
    smem = pl.BlockSpec(memory_space=pltpu.SMEM)
    return pl.pallas_call(
        kernel,
        in_specs=[smem, anywhere]
        + [pl.BlockSpec(memory_space=pltpu.VMEM)] * len(values),
        out_specs=anywhere,
        out_shape=shape(whole.shape, whole.dtype),
        input_output_aliases={1: 0},
        scratch_shapes=list(scratch) + [pltpu.SemaphoreType.DMA((4,))],
        compiler_params=pltpu.CompilerParams(vmem_limit_bytes=16 * 1024 * 1024),
        cost_estimate=pl.CostEstimate(
            flops=0, bytes_accessed=4 * 1024 * 1024, transcendentals=0
        ),
        name=name,
    )(meta, whole, *values)


def put_expert(k, whole, meta, mine, other):
    chips, rows, rank = mine.shape[-3:]

    def kernel(meta_ref, unused, mine_ref, other_ref, out_ref, new_ref, sems):
        parity = meta_ref[k, 2]

        def copy(part, size):
            at = pl.ds(part * size, size)
            return pltpu.make_async_copy(
                new_ref.at[at, :], out_ref.at[meta_ref[k, 1], at, :], sems.at[part]
            )

        for first in range(2):

            @pl.when((meta_ref[k, 0] == 1) & (meta_ref[k, 3] == first))
            def _():
                refs = (mine_ref, other_ref)
                if len(mine.shape) == 4:
                    refs = (mine_ref.at[parity], other_ref.at[parity])
                scale_halves(
                    refs[first],
                    refs[1 - first],
                    new_ref,
                    sent=lambda part, size: copy(part, size).start(),
                )
                for part in range(4):
                    copy(part, 2 * chips * rows // 4).wait()

    scratch = (pltpu.VMEM((2 * chips * rows, rank), BF16),)
    return put(kernel, "put_expert", whole, meta, (mine, other), scratch)


def blank(place, dims):
    def kernel(unused, out_ref, zero_ref, sems):
        zero_ref[...] = jnp.zeros_like(zero_ref)
        copies = [
            pltpu.make_async_copy(zero_ref, out_ref.at[i], sems.at[i])
            for i in range(dims[0])
        ]
        for copy in copies:
            copy.start()
        for copy in copies:
            copy.wait()

    return pl.pallas_call(
        kernel,
        in_specs=[pl.BlockSpec(memory_space=pltpu.SMEM)],
        out_specs=pl.BlockSpec(memory_space=pl.ANY),
        out_shape=shape(dims, BF16),
        scratch_shapes=[pltpu.VMEM(dims[1:], BF16), pltpu.SemaphoreType.DMA((dims[0],))],
        compiler_params=pltpu.CompilerParams(vmem_limit_bytes=16 * 1024 * 1024),
        cost_estimate=pl.CostEstimate(
            flops=0, bytes_accessed=8 * 1024 * 1024, transcendentals=0
        ),
        name="blank",
    )(place)


def swap_core(x):
    return lax.ppermute(x, "core", [(0, 1), (1, 0)])


def shift(x, axis, k):
    n = lax.axis_size(axis)
    return lax.ppermute(x, axis, [(i, (i + k) % n) for i in range(n)])


def around(x, axis):
    far = {k: shift(x, axis, k) for k in (2, 1, 3)}
    return [x] + [far[k] for k in (1, 2, 3)]


def gather_plane(x, beside=()):
    half = x.shape[1] // 2
    first = jnp.stack(around(x[:, :half], "x"))
    second = jnp.stack(around(x[:, half:], "y"))
    first, second, beside = lax.optimization_barrier((first, second, beside))
    return around(first, "y") + around(second, "x"), beside


def local(momentum, gradient, qfactor, owner_of):
    groups = lax.axis_size("grp")
    chips = lax.axis_size(PLANE)
    homed, rows_local, width = momentum.shape
    owned, unused, rank = qfactor.shape
    total = owner_of.shape[0]
    group = lax.axis_index("grp")
    core = lax.axis_index("core")
    chip = lax.axis_index(PLANE)
    place = jnp.stack([lax.axis_index("y"), lax.axis_index("x"), core]).astype(jnp.int32)

    index = jnp.arange(total, dtype=jnp.int32)
    same = owner_of[:, None] == owner_of[None, :]
    earlier = index[None, :] < index[:, None]
    slot = jnp.sum((same & earlier).astype(jnp.int32), axis=1)
    hops = jnp.arange(groups, dtype=jnp.int32)
    after = (group + hops) % groups
    before = (group - hops + groups) % groups
    slots = jnp.arange(owned, dtype=jnp.int32)
    house = index // homed
    in_slot = (slot[:, None] == slots[None, :]) & (owner_of == group)[:, None]
    this_core = index % homed == core

    share = width // chips
    held = lax.dynamic_slice(qfactor, (0, chip * share, 0), (owned, share, rank))
    goes = (house[None, :] == after[:, None]) & this_core[None, :]
    goes = jnp.any(goes[:, :, None] & in_slot[None, :, :], axis=1)
    comes = (house == group) & this_core
    comes = jnp.any(comes[None, :] & (owner_of[None, :] == before[:, None]), axis=1)
    pieces = []
    for k in range(groups):
        piece = jnp.sum(jnp.where(goes[k][:, None, None], held, 0), axis=0, dtype=BF16)
        pieces.append(shift(piece, "grp", k) if k > 0 else piece)
    right = jnp.sum(
        jnp.where(comes[:, None, None], jnp.stack(pieces), 0), axis=0, dtype=BF16
    )
    pieces, unused = gather_plane(right)

    blended = (momentum_decay * momentum.astype(F32) + gradient.astype(F32)).astype(BF16)
    keep = jnp.where(core == 0, blended[0], blended[1])
    give = jnp.where(core == 0, blended[1], blended[0])
    blocks = (keep, swap_core(give))

    projs, packed = project(place, *blocks, pieces)

    parts = packed.reshape(chips, packed.shape[0] // chips, BLOCK)
    part = jnp.sum(lax.all_to_all(parts, PLANE, 0, 0, tiled=True), axis=0)
    many = jnp.broadcast_to(part[None], (chips,) + part.shape)
    gram = lax.all_to_all(many, PLANE, 0, 0, tiled=True)
    inverse = inverse_factor(gram.reshape(-1, BLOCK), rank)

    bases, terms = partial(inverse, blocks, projs)
    terms = lax.all_to_all(terms, PLANE, 0, 0, tiled=True)
    rounded = jnp.sum(terms.astype(F32), axis=0).astype(BF16)

    half = share // 2
    lower, upper = rounded[:half], rounded[half:]
    stay = jnp.where(core == 0, lower, upper)
    other = swap_core(jnp.where(core == 0, upper, lower))
    both = jnp.concatenate(
        [jnp.where(core == 0, stay, other), jnp.where(core == 0, other, stay)], axis=0
    )

    theirs = (house == group)[None, :] & (owner_of[None, :] == after[:, None])
    theirs = jnp.any(theirs & (index % homed == 0)[None, :], axis=1)
    taken = (house[None, :] == before[:, None]) & (owner_of == group)[None, :]
    meta = jnp.stack(
        [
            jnp.any(taken, axis=1).astype(jnp.int32),
            jnp.sum(jnp.where(taken, slot[None, :], 0), axis=1, dtype=jnp.int32),
            jnp.sum(jnp.where(taken, index[None, :] % homed, 0), axis=1, dtype=jnp.int32),
            jnp.broadcast_to(core, (groups,)).astype(jnp.int32),
        ],
        axis=1,
    )
    piece = jnp.where(theirs[2:3, None], both[:half], both[half:])
    pieces, piece = gather_plane(both, shift(piece, "grp", 2))
    whole = blank(place, (owned, width, rank))
    pieces, whole = lax.optimization_barrier((pieces, whole))
    many = jnp.broadcast_to(piece[None], (chips, half, rank))
    many = lax.all_to_all(many, PLANE, 0, 0, tiled=True)
    both, *sends = split(place, theirs.astype(jnp.int32), pieces, homed)
    came = [shift(send, "grp", k) for send, k in zip(sends, (1, 3))]
    facing = swap_core(both)
    full, fresh = scale(place, both, facing)
    whole = put_expert(0, whole, meta, both, facing)
    full, whole = lax.optimization_barrier((full, whole))
    factor = math.sqrt(2 * rows_local * chips * width / rank)
    kept, moved = finish(factor, place, full, fresh, blocks, bases)
    many, came, kept, moved = lax.optimization_barrier((many, came, kept, moved))
    outs = [put_rows(own, place, swap_core(give)) for own, give in zip(kept, moved)]
    whole = put_expert(2, whole, meta, many, swap_core(many))
    for k, value in zip((1, 3), came):
        whole = put_expert(k, whole, meta, value, swap_core(value))
    new_qfactor = whole

    return (*outs, new_qfactor)


def solution(mesh):
    fine = Mesh(mesh.devices.reshape(4, 4, 4, 2), ("grp", "y", "x", "core"))
    rows = P("grp", ROWS, None)
    return jax.shard_map(
        local,
        mesh=fine,
        in_specs=(rows, rows, P("grp", None, None), P()),
        out_specs=(rows, rows, P("grp", None, None)),
        check_vma=False,
    )
```
